768 devices in a mesh: dp: 96 (over x, z, core), expert: 8 (over y).
Axes of the slice: x: 4, y: 8, z: 12, core: 2. Of those that a mesh axis runs over, the one named last changes fastest.
Arguments:
- normed_input: bfloat16 [98304, 3584], P(('dp', 'expert')), may hold values from -6 to 6
- output_grad: bfloat16 [98304, 3584], P(('dp', 'expert')), may hold values from -4 to 4
- route_logits: float32 [98304, 2], P(('dp', 'expert')), may hold values from -6 to 6
- route_ids: int32 [98304, 2], P(('dp', 'expert')), may hold values from 0 to 7, all different within a row; in each aligned block of 128 rows (0 to 127, 128 to 255, ...) at most 36 rows name the same one
- down_weight: bfloat16 [8, 1024, 3584], P('expert'), may hold values from -0.1875 to 0.1875
- pre_act: bfloat16 [221184, 2048], P(('dp', 'expert')), may hold values from -6 to 6
Outputs:
- pre_grad: bfloat16 [221184, 2048], P(('dp', 'expert'))
- router_grad: float32 [8, 3584], P('expert')
The draws below stay inside these ranges and needn't reach their ends.
Inputs may be any that keep to these rules, and one draw needn't show every extreme that they name: `route_ids`: each row names 2 different experts. Among the rows of one device no expert is named more than 36 times, a bound that some block reaches.
All inputs are finite; a program needn't handle non-finite values.
Results may differ from the reference program's by a relative error of at most 0.008.
Values may be sent and summed in bfloat16 or wider, within the bound.
A program may use at most 64 MiB of HBM per device.

```python
import math
import jax
import jax.numpy as jnp
import numpy as np
from jax import lax

D = 3584
FF = 1024
TOP = 2
TOK_DEV = 128
EXPERTS = 8
CAP = 36
TOKENS = 98304
N_DP = 96
N_EXPERT = 8


def block_levels(rng, dims, pieces, low, top_value):
    level = 1.0
    for axis_at, shards_of in pieces:
        steps = jax.random.uniform(jax.random.fold_in(jax.random.fold_in(rng, 6), axis_at), (shards_of,), jnp.float32, low / len(pieces), top_value / len(pieces))
        level = level * jnp.repeat(jnp.exp(steps), dims[axis_at] // shards_of).reshape((-1,) + (1,) * (len(dims) - 1 - axis_at))
    return level


def assign_block(key, own, number, rows, number_of, top, reach, lean):
    ranking = jax.random.permutation(key, number_of)
    heavy_load, usual = portions_of(number_of, rows * top, reach, lean, True), portions_of(number_of, rows * top, reach, lean, False)
    places = jnp.arange(number_of)

    def named(tallies, rotation):
        used = int((tallies > 0).sum())
        fixed = max(1, used // 4)
        passed = fixed + (places - fixed + rotation * (used - fixed)) % max(1, number_of - fixed)
        return jnp.zeros((number_of,), jnp.int32).at[ranking[jnp.where(places < fixed, places, passed)]].set(jnp.asarray(tallies, jnp.int32))

    tallies = jnp.where(number % 4 == 0, named(heavy_load, number // 4), named(usual, number - number // 4 - 1))
    mixed = jax.random.permutation(jax.random.fold_in(own, 3), number_of)
    source_of, receiver = mixed[0:number_of // 2 * 2:2], mixed[1:number_of // 2 * 2:2]
    room = jnp.minimum(tallies[source_of] - 1, reach - tallies[receiver]) // 2
    room = jnp.where((source_of == ranking[0]) | (receiver == ranking[0]) | (tallies[receiver] == 0), 0, jnp.maximum(room, 0))
    passed = jax.random.randint(jax.random.fold_in(own, 4), (number_of // 2,), 0, 1 << 20) % (room + 1)
    tallies = tallies.at[source_of].add(-passed).at[receiver].add(passed)
    items = jnp.searchsorted(jnp.cumsum(tallies), jnp.arange(rows * top), side="right").astype(jnp.int32)
    table = items.reshape(top, rows).T
    table = table[jax.random.permutation(jax.random.fold_in(own, 1), rows)]
    rotation = jax.random.randint(jax.random.fold_in(own, 2), (rows, 1), 0, top)
    return jnp.take_along_axis(table, (jnp.arange(top)[None, :] + rotation) % top, axis=1)


def portions_of(number_of, total, reach, slope, full):
    loads = [(1 << 20) // math.isqrt(rank ** slope) + 1 for rank in range(1, number_of + 1)]
    largest = reach if full else min(reach, max(-(-total // number_of), total * loads[0] // sum(loads)))
    least = 1 if total - largest >= number_of - 1 else 0
    holding, rest = [largest] + [least] * (number_of - 1), total - largest - least * (number_of - 1)
    while rest > 0:
        candidates = [i for i in range(1, number_of) if holding[i] < largest] or [i for i in range(1, number_of) if holding[i] < reach]
        whole, budget = sum([loads[i] for i in candidates]), rest
        for i in candidates:
            addition = min(reach - holding[i], max(1, budget * loads[i] // whole), rest)
            holding[i] = holding[i] + addition
            rest = rest - addition
    return np.array(holding)


def normal_values(rng, dims, width, reach, pieces=(), held_as=jnp.bfloat16):
    values = width * jax.random.normal(rng, dims, jnp.float32)
    if pieces:
        values = values * block_levels(rng, dims, pieces, -0.22, 0.18)
    return jnp.clip(values, -reach, reach).astype(held_as)


def setup_inputs(seed: int = 0) -> dict:
    arg_keys = jax.random.split(jax.random.key(seed), 7)
    normed_input = normal_values(arg_keys[0], (TOKENS, D), 1.0, 6.0, ((0, 768),))
    output_grad = normal_values(arg_keys[1], (TOKENS, D), 0.5, 4.0, ((0, 768),))
    route_logits = normal_values(arg_keys[2], (TOKENS, TOP), 1.5, 6.0, ((0, 768),), jnp.float32)
    route_ids_keys = jax.random.split(jax.random.fold_in(arg_keys[3], 1), TOKENS // TOK_DEV)
    route_ids_turns = jax.random.permutation(jax.random.fold_in(arg_keys[3], 3), TOKENS // TOK_DEV)
    route_ids = jax.vmap(lambda own, number: assign_block(jax.random.fold_in(arg_keys[3], 2), own, number, TOK_DEV, EXPERTS, TOP, CAP, 2))(route_ids_keys, route_ids_turns).reshape((TOKENS, TOP))
    down_weight = normal_values(arg_keys[4], (EXPERTS, FF, D), FF ** -0.5, 0.1875, ((0, 8),))
    pre_act = normal_values(arg_keys[5], (N_DP * N_EXPERT * N_EXPERT * CAP, 2 * FF), 1.0, 6.0, ((0, 768),))
    return dict(normed_input=normed_input, output_grad=output_grad, route_logits=route_logits, route_ids=route_ids, down_weight=down_weight, pre_act=pre_act)


def reference(normed_input, output_grad, route_logits, route_ids, down_weight, pre_act):
    route_count = TOK_DEV * TOP
    slot_count = N_EXPERT * CAP
    input_all = normed_input.reshape(N_DP, N_EXPERT, TOK_DEV, D)
    cotan_all = output_grad.reshape(N_DP, N_EXPERT, TOK_DEV, D)
    logit_all = route_logits.reshape(N_DP, N_EXPERT, TOK_DEV, TOP)
    ident_all = route_ids.reshape(N_DP, N_EXPERT, route_count)
    saved_all = pre_act.reshape(N_DP, N_EXPERT, slot_count, 2 * FF)

    def expert_work(members):
        in_rows, in_gates, saved, weight_mat = members
        gate_pre = saved[:, :FF].astype(jnp.float32)
        up_pre = saved[:, FF:].astype(jnp.float32)
        sigmoid_gate = jax.nn.sigmoid(gate_pre)
        hidden = (gate_pre * sigmoid_gate * up_pre).astype(jnp.bfloat16)
        expert_out = jnp.dot(hidden, weight_mat, preferred_element_type=jnp.float32).astype(jnp.bfloat16)
        products = lax.optimization_barrier(jnp.sum(expert_out.astype(jnp.float32) * in_rows.astype(jnp.float32), axis=-1))
        back_grad = jnp.dot(in_rows, weight_mat.T, preferred_element_type=jnp.float32) * in_gates.astype(jnp.float32)[:, None]
        gate_grad = back_grad * up_pre * sigmoid_gate * (1.0 + gate_pre * (1.0 - sigmoid_gate))
        up_grad = back_grad * gate_pre * sigmoid_gate
        return (jnp.concatenate([gate_grad, up_grad], axis=-1).astype(jnp.bfloat16), products)

    def group_work(members):
        group_input, group_cotan, group_logit, group_ident, group_saved = members
        scores = jax.nn.sigmoid(group_logit)
        total_score = lax.optimization_barrier(jnp.sum(scores, axis=-1, keepdims=True))
        weight = scores / total_score
        onehot = (group_ident[..., None] == jnp.arange(N_EXPERT, dtype=jnp.int32)).astype(jnp.int32)
        earlier = jnp.cumsum(onehot, axis=1) - onehot
        slot_index = lax.optimization_barrier(jnp.sum(earlier * onehot, axis=-1))
        position = (group_ident * CAP + slot_index).astype(jnp.int32)
        placing = (position[:, None, :] == jnp.arange(slot_count, dtype=jnp.int32)[None, :, None]).astype(jnp.float32)
        placing_tok = placing.reshape(N_EXPERT, slot_count, TOK_DEV, TOP).sum(-1)
        send_rows = jnp.einsum('spt,std->spd', placing_tok, group_cotan.astype(jnp.float32)).astype(jnp.bfloat16)
        gate_send = weight.astype(jnp.bfloat16).astype(jnp.float32).reshape(N_EXPERT, route_count)
        send_gates = jnp.einsum('spr,sr->sp', placing, gate_send).astype(jnp.bfloat16)
        in_rows = send_rows.reshape(N_EXPERT, N_EXPERT, CAP, D).transpose(1, 0, 2, 3).reshape(N_EXPERT, slot_count, D)
        in_gates = send_gates.reshape(N_EXPERT, N_EXPERT, CAP).transpose(1, 0, 2).reshape(N_EXPERT, slot_count)
        slot_grad, products = lax.map(expert_work, (in_rows, in_gates, group_saved, down_weight))
        products_src = products.reshape(N_EXPERT, N_EXPERT, CAP).transpose(1, 0, 2).reshape(N_EXPERT, slot_count)
        route_prod = jnp.take_along_axis(products_src, position, axis=1).reshape(N_EXPERT, TOK_DEV, TOP)
        mixture = lax.optimization_barrier(jnp.sum(weight * route_prod, axis=-1, keepdims=True))
        logit_grad = (route_prod - mixture) / total_score * scores * (1.0 - scores)
        router_terms = jnp.einsum('str,stre->ste', logit_grad, onehot.reshape(N_EXPERT, TOK_DEV, TOP, N_EXPERT).astype(jnp.float32))
        router_part = jnp.einsum('ste,std->ed', router_terms, group_input.astype(jnp.float32), precision=lax.Precision.HIGHEST)
        return (slot_grad, router_part)
    slot_grad, router_parts = lax.map(group_work, (input_all, cotan_all, logit_all, ident_all, saved_all))
    pre_grad = slot_grad.reshape(N_DP * N_EXPERT * slot_count, 2 * FF)
    router_grad = lax.optimization_barrier(jnp.sum(router_parts, axis=0)) * (1.0 / math.sqrt(TOKENS))
    return (pre_grad, router_grad)
```

```python
import functools
import math

import jax
import jax.numpy as jnp
from jax import lax
from jax.experimental import pallas as pl
from jax.experimental.pallas import tpu as pltpu
from jax.sharding import PartitionSpec as P

MESH = pl.DeviceIdType.MESH
F32 = jnp.float32
BF16 = jnp.bfloat16
MAIN = 32
WIDE = 128


def dot(a, b):
    return jnp.dot(a, b, preferred_element_type=F32)


def dp_dims(n_dp):
    return (4, n_dp // 8, 2)


def kernel(
    dims,
    groups,
    cap,
    ids_ref,
    logits_ref,
    x_hbm,
    g_hbm,
    w_hbm,
    pre_hbm,
    out_hbm,
    router_ref,
    g_v,
    x_v,
    w_v,
    pre_v,
    send,
    recv,
    lhs,
    acc,
    hid,
    gfac,
    ufac,
    out_v,
    gate_send,
    gate_recv,
    c_sum,
    c_send,
    c_recv,
    y_send,
    y_recv,
    g_send,
    g_recv,
    z_send,
    z_recv,
    f_recv,
    load_sem,
    out_sem,
    send_sem,
    recv_sem,
    self_sem,
    gate_ss,
    gate_rs,
    c_ss,
    c_rs,
    y_ss,
    y_rs,
    g_ss,
    g_rs,
    z_ss,
    z_rs,
    f_ss,
    f_rs,
):
    nx, nz, nc = dims
    team = nx * nc
    tokens, width = g_v.shape
    ff = w_v.shape[0]
    extra = cap - MAIN
    tiles = 16 // extra
    chunk = tiles * WIDE
    chunks = width // chunk
    rows_main = groups * MAIN
    rows_all = groups * cap
    piece = z_send.shape[-1]

    q = lax.axis_index("dp")
    me = lax.axis_index("expert")
    core = lax.rem(q, nc)
    zi = lax.rem(q // nc, nz)
    xi = q // (nc * nz)
    rank = xi * nc + core

    def ring(d):
        return lax.rem(me + d, groups)

    def mate(d):
        r = lax.rem(rank + d, team)
        return ((r // nc) * nz + zi) * nc + lax.rem(r, nc), r

    def zmate(d):
        z = lax.rem(zi + d, nz)
        return (xi * nz + z) * nc + core, z

    loads = [
        pltpu.make_async_copy(g_hbm, g_v, load_sem.at[0]),
        pltpu.make_async_copy(pre_hbm, pre_v, load_sem.at[1]),
        pltpu.make_async_copy(w_hbm.at[0], w_v, load_sem.at[2]),
        pltpu.make_async_copy(x_hbm, x_v, load_sem.at[3]),
    ]
    for one in loads:
        one.start()

    barrier = pltpu.get_barrier_semaphore()
    for d in range(1, groups):
        pl.semaphore_signal(barrier, inc=1, device_id=(q, ring(d)), device_id_type=MESH)
    for d in range(1, team):
        pl.semaphore_signal(barrier, inc=1, device_id=(mate(d)[0], me), device_id_type=MESH)
    for d in range(1, nz):
        pl.semaphore_signal(barrier, inc=1, device_id=(zmate(d)[0], me), device_id_type=MESH)

    ids = ids_ref[...].astype(F32)
    logits = logits_ref[...]
    scores = jax.nn.sigmoid(logits)
    score = [scores[:, k : k + 1] for k in range(2)]
    total = score[0] + score[1]
    weight = [s / total for s in score]
    lane = lax.broadcasted_iota(jnp.int32, (tokens, WIDE), 1).astype(F32)
    ident = [ids[:, k : k + 1] for k in range(2)]
    onehot = [(i == lane).astype(F32) for i in ident]
    earlier = (
        lax.broadcasted_iota(jnp.int32, (tokens, tokens), 1)
        < lax.broadcasted_iota(jnp.int32, (tokens, tokens), 0)
    ).astype(F32)
    count = dot(earlier.astype(BF16), (onehot[0] + onehot[1]).astype(BF16))
    slot = [jnp.sum(o * count, axis=1, keepdims=True) for o in onehot]
    packed = jnp.zeros((tokens, WIDE), F32)
    for k in range(2):
        inside = slot[k] < MAIN
        p_main = jnp.where(inside, ident[k] * MAIN + slot[k], -1.0)
        p_extra = jnp.where(inside, -1000.0, ident[k] * 16 + slot[k] - MAIN)
        packed = jnp.where(lane == k, p_main, packed)
        packed = jnp.where(lane == 2 + k, p_extra, packed)
    turned = jnp.transpose(packed)
    row_main = lax.broadcasted_iota(jnp.int32, (rows_main, tokens), 0).astype(F32)
    row_extra = lax.broadcasted_iota(jnp.int32, (groups * 16, tokens), 0).astype(F32)
    place_main = (
        (row_main == turned[0:1]).astype(F32) + (row_main == turned[1:2]).astype(F32)
    ).astype(BF16)
    place_extra = [
        (
            (row_extra == turned[2:3] + extra * t).astype(F32)
            + (row_extra == turned[3:4] + extra * t).astype(F32)
        ).astype(BF16)
        for t in range(tiles)
    ]
    gates = jnp.zeros((WIDE, WIDE), F32)
    for k in range(2):
        held = jnp.where(lane == slot[k], weight[k].astype(BF16).astype(F32), 0.0)
        gates = gates + dot(jnp.transpose(onehot[k]).astype(BF16), held.astype(BF16))
    for e in range(groups):
        gate_send[e] = gates[e : e + 1]

    order = sorted(range(1, groups), key=lambda d: -min(d, groups - d))

    def gate_copy(d):
        to = ring(d)
        return pltpu.make_async_remote_copy(
            src_ref=gate_send.at[to],
            dst_ref=gate_recv.at[me],
            send_sem=gate_ss.at[d],
            recv_sem=gate_rs.at[me],
            device_id=(q, to),
            device_id_type=MESH,
        )

    def row_copy(k, d):
        to = ring(d)
        return pltpu.make_async_remote_copy(
            src_ref=send.at[k, to],
            dst_ref=recv.at[k, me],
            send_sem=send_sem.at[k, d],
            recv_sem=recv_sem.at[k, me],
            device_id=(q, to),
            device_id_type=MESH,
        )

    def self_copy(k):
        return pltpu.make_async_copy(send.at[k, me], recv.at[k, me], self_sem.at[k])

    def arrived(buffer, sem):
        pltpu.make_async_copy(buffer, buffer, sem).wait()

    loads[0].wait()
    pl.semaphore_wait(barrier, groups - 1 + team - 1 + nz - 1)
    for d in order:
        gate_copy(d).start()
    gate_recv[me] = gate_send[me]

    def send_chunk(k, carry):
        cols = g_v[:, pl.ds(pl.multiple_of(k * chunk, chunk), chunk)]
        main = dot(place_main, cols).astype(BF16)
        rest = jnp.zeros((groups * 16, WIDE), F32)
        for t in range(tiles):
            piece_t = main[:, t * WIDE : (t + 1) * WIDE]
            send[k, :, t * MAIN : (t + 1) * MAIN, :] = piece_t.reshape(groups, MAIN, WIDE)
            rest = rest + dot(place_extra[t], cols[:, t * WIDE : (t + 1) * WIDE])
        send[k, :, tiles * MAIN :, :] = rest.astype(BF16).reshape(groups, 16, WIDE)
        for d in order:
            row_copy(k, d).start()
        self_copy(k).start()
        return carry

    lax.fori_loop(0, chunks, send_chunk, 0)

    for d in range(1, groups):
        arrived(gate_recv.at[ring(d)], gate_rs.at[ring(d)])
    lane_m = lax.broadcasted_iota(jnp.int32, (MAIN, WIDE), 1)
    row_m = lax.broadcasted_iota(jnp.int32, (MAIN, WIDE), 0)
    rows_x = rows_all - rows_main
    lane_x = lax.broadcasted_iota(jnp.int32, (rows_x, WIDE), 1)
    row_x = lax.broadcasted_iota(jnp.int32, (rows_x, WIDE), 0)
    gate_x = jnp.zeros((rows_x, WIDE), F32)
    gate_parts = []
    for j in range(groups):
        one = gate_recv[j]
        gate_parts.append(
            jnp.sum(jnp.where(lane_m == row_m, one, 0.0), axis=1, keepdims=True)
        )
        mine = (row_x // extra == j) & (lane_x == MAIN + row_x % extra)
        gate_x = gate_x + jnp.where(mine, one, 0.0)
    gate_parts.append(jnp.sum(gate_x, axis=1, keepdims=True))
    gate_col = jnp.concatenate(gate_parts, axis=0)

    def natural(r):
        s = r - rows_main
        return jnp.where(
            r < rows_main,
            (r // MAIN) * cap + r % MAIN,
            (s // extra) * cap + MAIN + s % extra,
        )

    square_r = lax.broadcasted_iota(jnp.int32, (rows_all, rows_all), 0)
    square_c = lax.broadcasted_iota(jnp.int32, (rows_all, rows_all), 1)
    to_mine = (natural(square_r) == square_c).astype(F32).astype(BF16)
    to_natural = (natural(square_c) == square_r).astype(F32).astype(BF16)
    loads[1].wait()
    block = 256

    def prepare(n, carry):
        at = pl.ds(pl.multiple_of(n * block, block), block)
        at_up = pl.ds(pl.multiple_of(ff + n * block, block), block)
        g = dot(to_mine, pre_v[:, at])
        u = dot(to_mine, pre_v[:, at_up])
        s = jax.nn.sigmoid(g)
        gs = g * s
        hid[:, at] = (gs * u).astype(BF16)
        gfac[:, at] = gate_col * u * s * (1.0 + g * (1.0 - s))
        ufac[:, at] = gate_col * gs
        return carry

    lax.fori_loop(0, ff // block, prepare, 0)
    acc[...] = jnp.zeros_like(acc)
    pick = []
    for t in range(tiles):
        r = lax.broadcasted_iota(jnp.int32, (rows_x, groups * 16), 0)
        c = lax.broadcasted_iota(jnp.int32, (rows_x, groups * 16), 1)
        pick.append(
            ((r // extra) * 16 + t * extra + r % extra == c).astype(F32).astype(BF16)
        )
    loads[2].wait()

    def use_chunk(k, carry):
        self_copy(k).wait()
        for d in range(1, groups):
            arrived(recv.at[k, ring(d)], recv_sem.at[k, ring(d)])
        rest = recv[k, :, tiles * MAIN :, :].reshape(groups * 16, WIDE)
        for t in range(tiles):
            at = slice(t * WIDE, (t + 1) * WIDE)
            lhs[0:rows_main, at] = recv[k, :, t * MAIN : (t + 1) * MAIN, :].reshape(
                rows_main, WIDE
            )
            lhs[rows_main:, at] = dot(pick[t], rest).astype(BF16)
        kat = pl.ds(pl.multiple_of(k * chunk, chunk), chunk)

        def tile(n, inner):
            at = pl.ds(pl.multiple_of(n * block, block), block)
            acc[:, at] += lax.dot_general(
                lhs[...], w_v[at, kat], (((1,), (1,)), ((), ())), preferred_element_type=F32
            )
            return inner

        return lax.fori_loop(0, ff // block, tile, carry)

    lax.fori_loop(0, chunks, use_chunk, 0)

    c_sum[...] = jnp.zeros_like(c_sum)
    summed = jnp.zeros((rows_all, WIDE), F32)
    for n in range(ff // WIDE):
        at = slice(n * WIDE, (n + 1) * WIDE)
        summed = summed + hid[:, at].astype(F32) * acc[:, at]
    c_sum[0:rows_all] = summed
    c_send[...] = jnp.sum(jnp.transpose(c_sum[...]), axis=0, keepdims=True)
    c_recv[me] = c_send[...]

    def c_copy(d):
        return pltpu.make_async_remote_copy(
            src_ref=c_send,
            dst_ref=c_recv.at[me],
            send_sem=c_ss.at[d],
            recv_sem=c_rs.at[me],
            device_id=(q, ring(d)),
            device_id_type=MESH,
        )

    for d in order:
        c_copy(d).start()

    def finish(n, carry):
        at = pl.ds(pl.multiple_of(n * block, block), block)
        at_up = pl.ds(pl.multiple_of(ff + n * block, block), block)
        back = acc[:, at]
        out_v[:, at] = dot(to_natural, (back * gfac[:, at]).astype(BF16)).astype(BF16)
        out_v[:, at_up] = dot(to_natural, (back * ufac[:, at]).astype(BF16)).astype(BF16)
        return carry

    lax.fori_loop(0, ff // block, finish, 0)
    out_copy = pltpu.make_async_copy(out_v, out_hbm, out_sem)
    out_copy.start()

    for d in range(1, groups):
        arrived(c_recv.at[ring(d)], c_rs.at[ring(d)])
    c_wide = c_send.shape[-1]
    c_lane = lax.broadcasted_iota(jnp.int32, (tokens, c_wide), 1).astype(F32)
    me_f = me.astype(F32)
    prod = []
    for k in range(2):
        found = jnp.zeros((tokens, c_wide), F32)
        for e in range(groups):
            found = found + jnp.where(ident[k] == float(e), c_recv[e], 0.0)
        target = jnp.where(
            slot[k] < MAIN,
            me_f * MAIN + slot[k],
            rows_main + me_f * extra + slot[k] - MAIN,
        )
        prod.append(jnp.sum(jnp.where(c_lane == target, found, 0.0), axis=1, keepdims=True))
    mixture = weight[0] * prod[0] + weight[1] * prod[1]
    terms = jnp.zeros((tokens, WIDE), F32)
    for k in range(2):
        grad = (prod[k] - mixture) / total * score[k] * (1.0 - score[k])
        terms = terms + onehot[k] * grad
    terms = jnp.transpose(terms)[0:groups]
    high = terms.astype(BF16).astype(F32)
    middle = (terms - high).astype(BF16).astype(F32)
    low = terms - high - middle
    stack = jnp.concatenate([high, middle, low, jnp.zeros_like(low)], axis=0).astype(BF16)
    loads[3].wait()
    for n in range(chunks):
        at = slice(n * chunk, (n + 1) * chunk)
        three = dot(stack, x_v[:, at])
        part = three[0:groups] + three[groups : 2 * groups] + three[2 * groups : 3 * groups]
        for e in range(groups):
            y_send[e, :, at] = part[e : e + 1]

    def y_copy(d):
        to = ring(d)
        return pltpu.make_async_remote_copy(
            src_ref=y_send.at[to],
            dst_ref=y_recv.at[me],
            send_sem=y_ss.at[d],
            recv_sem=y_rs.at[me],
            device_id=(q, to),
            device_id_type=MESH,
        )

    for d in order:
        y_copy(d).start()
    y_recv[me] = y_send[me]
    for d in range(1, groups):
        arrived(y_recv.at[ring(d)], y_rs.at[ring(d)])

    mine = y_recv[0]
    for j in range(1, groups):
        mine = mine + y_recv[j]
    for i in range(team):
        low_at, high_at = i * piece, min((i + 1) * piece, width)
        if high_at - low_at < piece:
            g_send[i] = jnp.zeros((1, piece), F32)
        if high_at > low_at:
            g_send[i, :, 0 : high_at - low_at] = mine[:, low_at:high_at]

    def g_copy(d):
        to, r = mate(d)
        return pltpu.make_async_remote_copy(
            src_ref=g_send.at[r],
            dst_ref=g_recv.at[rank],
            send_sem=g_ss.at[d],
            recv_sem=g_rs.at[rank],
            device_id=(to, me),
            device_id_type=MESH,
        )

    for d in range(1, team):
        g_copy(d).start()
    g_recv[rank] = g_send[rank]
    for d in range(1, team):
        arrived(g_recv.at[mate(d)[1]], g_rs.at[mate(d)[1]])
    mine = g_recv[0]
    for j in range(1, team):
        mine = mine + g_recv[j]
    z_send[...] = mine

    def z_copy(d):
        to, _ = zmate(d)
        return pltpu.make_async_remote_copy(
            src_ref=z_send,
            dst_ref=z_recv.at[zi],
            send_sem=z_ss.at[d],
            recv_sem=z_rs.at[zi],
            device_id=(to, me),
            device_id_type=MESH,
        )

    for d in sorted(range(1, nz), key=lambda d: -min(d, nz - d)):
        z_copy(d).start()
    z_recv[zi] = mine
    for d in range(1, nz):
        arrived(z_recv.at[zmate(d)[1]], z_rs.at[zmate(d)[1]])
    mine = z_recv[0]
    for j in range(1, nz):
        mine = mine + z_recv[j]
    f_recv[rank] = mine * (1.0 / math.sqrt(tokens * nx * nz * nc * groups))

    def f_copy(d):
        to, _ = mate(d)
        return pltpu.make_async_remote_copy(
            src_ref=f_recv.at[rank],
            dst_ref=f_recv.at[rank],
            send_sem=f_ss.at[d],
            recv_sem=f_rs.at[rank],
            device_id=(to, me),
            device_id_type=MESH,
        )

    for d in range(1, team):
        f_copy(d).start()
    for d in range(1, team):
        arrived(f_recv.at[mate(d)[1]], f_rs.at[mate(d)[1]])
    for i in range(team):
        low_at, high_at = i * piece, min((i + 1) * piece, width)
        if high_at > low_at:
            router_ref[:, low_at:high_at] = f_recv[i][:, 0 : high_at - low_at]

    def sent(k, carry):
        for d in order:
            row_copy(k, d).wait_send()
        return carry

    lax.fori_loop(0, chunks, sent, 0)
    for d in order:
        gate_copy(d).wait_send()
        c_copy(d).wait_send()
        y_copy(d).wait_send()
    for d in range(1, team):
        g_copy(d).wait_send()
        f_copy(d).wait_send()
    for d in range(1, nz):
        z_copy(d).wait_send()
    out_copy.wait()


def body(dims, normed_input, output_grad, route_logits, route_ids, down_weight, pre_act):
    groups = lax.axis_size("expert")
    tokens, width = normed_input.shape
    ff = down_weight.shape[1]
    slots = pre_act.shape[0]
    cap = slots // groups
    nx, nz, nc = dims
    team = nx * nc
    extra = cap - MAIN
    tiles = 16 // extra
    chunk = tiles * WIDE
    chunks = width // chunk
    block_rows = tiles * MAIN + 16
    piece = -(-width // (team * WIDE)) * WIDE
    c_wide = -(-slots // WIDE) * WIDE
    vmem = pl.BlockSpec(memory_space=pltpu.VMEM)
    anywhere = pl.BlockSpec(memory_space=pl.ANY)
    dma = pltpu.SemaphoreType.DMA
    return pl.pallas_call(
        functools.partial(kernel, dims, groups, cap),
        out_shape=(
            jax.ShapeDtypeStruct((slots, 2 * ff), BF16),
            jax.ShapeDtypeStruct((1, width), F32),
        ),
        in_specs=[vmem, vmem, anywhere, anywhere, anywhere, anywhere],
        out_specs=(anywhere, vmem),
        scratch_shapes=[
            pltpu.VMEM((tokens, width), BF16),
            pltpu.VMEM((tokens, width), BF16),
            pltpu.VMEM((ff, width), BF16),
            pltpu.VMEM((slots, 2 * ff), BF16),
            pltpu.VMEM((chunks, groups, block_rows, WIDE), BF16),
            pltpu.VMEM((chunks, groups, block_rows, WIDE), BF16),
            pltpu.VMEM((slots, chunk), BF16),
            pltpu.VMEM((slots, ff), F32),
            pltpu.VMEM((slots, ff), BF16),
            pltpu.VMEM((slots, ff), F32),
            pltpu.VMEM((slots, ff), F32),
            pltpu.VMEM((slots, 2 * ff), BF16),
            pltpu.VMEM((groups, 1, WIDE), F32),
            pltpu.VMEM((groups, 1, WIDE), F32),
            pltpu.VMEM((c_wide, WIDE), F32),
            pltpu.VMEM((1, c_wide), F32),
            pltpu.VMEM((groups, 1, c_wide), F32),
            pltpu.VMEM((groups, 1, width), F32),
            pltpu.VMEM((groups, 1, width), F32),
            pltpu.VMEM((team, 1, piece), F32),
            pltpu.VMEM((team, 1, piece), F32),
            pltpu.VMEM((1, piece), F32),
            pltpu.VMEM((nz, 1, piece), F32),
            pltpu.VMEM((team, 1, piece), F32),
            dma((4,)),
            dma,
            dma((chunks, groups)),
            dma((chunks, groups)),
            dma((chunks,)),
            dma((groups,)),
            dma((groups,)),
            dma((groups,)),
            dma((groups,)),
            dma((groups,)),
            dma((groups,)),
            dma((team,)),
            dma((team,)),
            dma((nz,)),
            dma((nz,)),
            dma((team,)),
            dma((team,)),
        ],
        compiler_params=pltpu.CompilerParams(
            collective_id=0, has_side_effects=True, vmem_limit_bytes=56 * 1024 * 1024
        ),
        cost_estimate=pl.CostEstimate(
            flops=2 * slots * width * ff, bytes_accessed=12 * 1024 * 1024, transcendentals=0
        ),
    )(route_ids, route_logits, normed_input, output_grad, down_weight, pre_act)


def solution(mesh):
    dims = dp_dims(mesh.shape["dp"])
    return jax.shard_map(
        functools.partial(body, dims),
        mesh=mesh,
        in_specs=(
            P(("dp", "expert"), None),
            P(("dp", "expert"), None),
            P(("dp", "expert"), None),
            P(("dp", "expert"), None),
            P("expert", None, None),
            P(("dp", "expert"), None),
        ),
        out_specs=(P(("dp", "expert"), None), P("expert", None)),
        check_vma=False,
    )
```

```python
import functools
import math

import jax
import jax.numpy as jnp
from jax import lax
from jax.experimental import pallas as pl
from jax.experimental.pallas import tpu as pltpu
from jax.sharding import PartitionSpec as P

MESH = pl.DeviceIdType.MESH
F32 = jnp.float32
BF16 = jnp.bfloat16
MAIN = 32
WIDE = 128


def dot(a, b):
    return jnp.dot(a, b, preferred_element_type=F32)


def dp_dims(n_dp):
    return (4, n_dp // 8, 2)


def kernel(
    dims,
    groups,
    cap,
    ids_hbm,
    logits_hbm,
    x_hbm,
    g_hbm,
    w_hbm,
    pre_hbm,
    out_hbm,
    router_ref,
    ids_ref,
    logits_ref,
    g_v,
    x_v,
    w_v,
    pre_v,
    send,
    recv,
    lhs,
    acc,
    hid,
    gfac,
    ufac,
    out_v,
    gate_send,
    gate_recv,
    c_sum,
    c_send,
    c_recv,
    y_full,
    y_send,
    y_recv,
    g_send,
    g_recv,
    z_send,
    z_recv,
    g_sem,
    load_sem,
    out_sem,
    send_sem,
    recv_sem,
    self_sem,
    gate_ss,
    gate_rs,
    c_ss,
    c_rs,
    y_ss,
    y_rs,
    g_ss,
    g_rs,
    z_ss,
    z_rs,
):
    nx, nz, nc = dims
    team = nx * nc
    tokens, width = g_v.shape
    ff = w_v.shape[0]
    extra = cap - MAIN
    tiles = 16 // extra
    chunk = tiles * WIDE
    chunks = width // chunk
    rows_main = groups * MAIN
    rows_all = groups * cap

    q = lax.axis_index("dp")
    me = lax.axis_index("expert")
    core = lax.rem(q, nc)
    zi = lax.rem(q // nc, nz)
    xi = q // (nc * nz)
    rank = xi * nc + core

    def ring(d):
        return lax.rem(me + d, groups)

    def mate(d):
        r = lax.rem(rank + d, team)
        return ((r // nc) * nz + zi) * nc + lax.rem(r, nc), r

    def zmate(d):
        z = lax.rem(zi + d, nz)
        return (xi * nz + z) * nc + core, z

    ids_load = pltpu.make_async_copy(ids_hbm, ids_ref, load_sem.at[3])
    logits_load = pltpu.make_async_copy(logits_hbm, logits_ref, load_sem.at[4])
    ids_load.start()
    g_loads = [
        pltpu.make_async_copy(
            g_hbm.at[:, k * chunk : (k + 1) * chunk],
            g_v.at[:, k * chunk : (k + 1) * chunk],
            g_sem.at[k],
        )
        for k in range(chunks)
    ]
    for one in g_loads:
        one.start()
    logits_load.start()

    barrier = pltpu.get_barrier_semaphore()
    for d in range(1, groups):
        pl.semaphore_signal(barrier, inc=1, device_id=(q, ring(d)), device_id_type=MESH)
    for d in range(1, team):
        pl.semaphore_signal(barrier, inc=1, device_id=(mate(d)[0], me), device_id_type=MESH)
    for d in range(1, nz):
        pl.semaphore_signal(barrier, inc=1, device_id=(zmate(d)[0], me), device_id_type=MESH)

    loads = [
        pltpu.make_async_copy(pre_hbm, pre_v, load_sem.at[0]),
        pltpu.make_async_copy(w_hbm.at[0], w_v, load_sem.at[1]),
        pltpu.make_async_copy(x_hbm, x_v, load_sem.at[2]),
    ]

    ids_load.wait()
    ids = ids_ref[...].astype(F32)
    expert = lax.broadcasted_iota(jnp.int32, (16, tokens), 0).astype(F32)
    onehot_t = [(ids[k : k + 1] == expert).astype(F32) for k in range(2)]
    before = (
        lax.broadcasted_iota(jnp.int32, (tokens, tokens), 0)
        < lax.broadcasted_iota(jnp.int32, (tokens, tokens), 1)
    ).astype(F32)
    count_t = dot((onehot_t[0] + onehot_t[1]).astype(BF16), before.astype(BF16))
    slot_t = [jnp.sum(o * count_t, axis=0, keepdims=True) for o in onehot_t]
    to_main, to_extra = [], []
    for k in range(2):
        inside = slot_t[k] < MAIN
        at_k = ids[k : k + 1]
        to_main.append(jnp.where(inside, at_k * MAIN + slot_t[k], -1.0))
        to_extra.append(jnp.where(inside, -1000.0, at_k * 16 + slot_t[k] - MAIN))
    row_main = lax.broadcasted_iota(jnp.int32, (rows_main, tokens), 0).astype(F32)
    row_extra = lax.broadcasted_iota(jnp.int32, (groups * 16, tokens), 0).astype(F32)
    place_main = (
        (row_main == to_main[0]).astype(F32) + (row_main == to_main[1]).astype(F32)
    ).astype(BF16)
    place_extra = [
        (
            (row_extra == to_extra[0] + extra * t).astype(F32)
            + (row_extra == to_extra[1] + extra * t).astype(F32)
        ).astype(BF16)
        for t in range(tiles)
    ]

    order = sorted(range(1, groups), key=lambda d: -min(d, groups - d))

    def gate_copy(d):
        to = ring(d)
        return pltpu.make_async_remote_copy(
            src_ref=gate_send.at[to],
            dst_ref=gate_recv.at[me],
            send_sem=gate_ss.at[d],
            recv_sem=gate_rs.at[me],
            device_id=(q, to),
            device_id_type=MESH,
        )

    def row_copy(k, d):
        to = ring(d)
        return pltpu.make_async_remote_copy(
            src_ref=send.at[k, to],
            dst_ref=recv.at[k, me],
            send_sem=send_sem.at[k, d],
            recv_sem=recv_sem.at[k, me],
            device_id=(q, to),
            device_id_type=MESH,
        )

    def self_copy(k):
        return pltpu.make_async_copy(send.at[k, me], recv.at[k, me], self_sem.at[k])

    def arrived(buffer, sem):
        pltpu.make_async_copy(buffer, buffer, sem).wait()

    def fill_chunk(k):
        cols = g_v[:, pl.ds(pl.multiple_of(k * chunk, chunk), chunk)]
        main = dot(place_main, cols).astype(BF16)
        rest = jnp.zeros((groups * 16, WIDE), F32)
        for t in range(tiles):
            piece_t = main[:, t * WIDE : (t + 1) * WIDE]
            send[k, :, t * MAIN : (t + 1) * MAIN, :] = piece_t.reshape(groups, MAIN, WIDE)
            rest = rest + dot(place_extra[t], cols[:, t * WIDE : (t + 1) * WIDE])
        send[k, :, tiles * MAIN :, :] = rest.astype(BF16).reshape(groups, 16, WIDE)

    def start_chunk(k):
        for d in order:
            row_copy(k, d).start()
        self_copy(k).start()

    g_loads[0].wait()
    fill_chunk(0)
    pl.semaphore_wait(barrier, groups - 1 + team - 1 + nz - 1)
    start_chunk(0)
    for one in loads:
        one.start()

    logits_load.wait()
    scores_t = jax.nn.sigmoid(logits_ref[...])
    score_t = [scores_t[k : k + 1] for k in range(2)]
    total_t = score_t[0] + score_t[1]
    weight_t = [v / total_t for v in score_t]
    slot_row = lax.broadcasted_iota(jnp.int32, (WIDE, tokens), 0).astype(F32)
    gates = jnp.zeros((16, WIDE), F32)
    for k in range(2):
        gate = weight_t[k].astype(BF16).astype(F32)
        gates = gates + lax.dot_general(
            (onehot_t[k] * gate).astype(BF16),
            (slot_row == slot_t[k]).astype(F32).astype(BF16),
            (((1,), (1,)), ((), ())),
            preferred_element_type=F32,
        )
    for e in range(groups):
        gate_send[e] = gates[e : e + 1]
    for d in order:
        gate_copy(d).start()
    gate_recv[me] = gate_send[me]

    def send_chunk(k, carry):
        at = pl.ds(pl.multiple_of(k * chunk, chunk), chunk)
        pltpu.make_async_copy(g_hbm.at[:, at], g_v.at[:, at], g_sem.at[k]).wait()
        fill_chunk(k)
        start_chunk(k)
        return carry

    lax.fori_loop(1, chunks, send_chunk, 0)

    rows = [ids[0:1], ids[1:2], *slot_t, *score_t, *weight_t, total_t]
    rows.append(jnp.zeros((WIDE - len(rows), tokens), F32))
    columns = jnp.transpose(jnp.concatenate(rows, axis=0))
    column = [columns[:, i : i + 1] for i in range(9)]
    ident, slot, score, weight, total = (
        column[0:2],
        column[2:4],
        column[4:6],
        column[6:8],
        column[8],
    )
    lane = lax.broadcasted_iota(jnp.int32, (tokens, WIDE), 1).astype(F32)
    onehot = [(i == lane).astype(F32) for i in ident]
    y_full[...] = jnp.zeros_like(y_full)

    for d in range(1, groups):
        arrived(gate_recv.at[ring(d)], gate_rs.at[ring(d)])
    lane_m = lax.broadcasted_iota(jnp.int32, (MAIN, WIDE), 1)
    row_m = lax.broadcasted_iota(jnp.int32, (MAIN, WIDE), 0)
    rows_x = rows_all - rows_main
    lane_x = lax.broadcasted_iota(jnp.int32, (rows_x, WIDE), 1)
    row_x = lax.broadcasted_iota(jnp.int32, (rows_x, WIDE), 0)
    gate_x = jnp.zeros((rows_x, WIDE), F32)
    gate_parts = []
    for j in range(groups):
        one = gate_recv[j]
        gate_parts.append(
            jnp.sum(jnp.where(lane_m == row_m, one, 0.0), axis=1, keepdims=True)
        )
        mine = (row_x // extra == j) & (lane_x == MAIN + row_x % extra)
        gate_x = gate_x + jnp.where(mine, one, 0.0)
    gate_parts.append(jnp.sum(gate_x, axis=1, keepdims=True))
    gate_col = jnp.concatenate(gate_parts, axis=0)

    def natural(r):
        s = r - rows_main
        return jnp.where(
            r < rows_main,
            (r // MAIN) * cap + r % MAIN,
            (s // extra) * cap + MAIN + s % extra,
        )

    square_r = lax.broadcasted_iota(jnp.int32, (rows_all, rows_all), 0)
    square_c = lax.broadcasted_iota(jnp.int32, (rows_all, rows_all), 1)
    to_mine = (natural(square_r) == square_c).astype(F32).astype(BF16)
    to_natural = (natural(square_c) == square_r).astype(F32).astype(BF16)
    loads[0].wait()
    block = 256

    def prepare(n, carry):
        at = pl.ds(pl.multiple_of(n * block, block), block)
        at_up = pl.ds(pl.multiple_of(ff + n * block, block), block)
        g = dot(to_mine, pre_v[:, at])
        u = dot(to_mine, pre_v[:, at_up])
        s = jax.nn.sigmoid(g)
        gs = g * s
        hid[:, at] = (gs * u).astype(BF16)
        gfac[:, at] = gate_col * u * s * (1.0 + g * (1.0 - s))
        ufac[:, at] = gate_col * gs
        return carry

    lax.fori_loop(0, ff // block, prepare, 0)
    acc[...] = jnp.zeros_like(acc)
    pick = []
    for t in range(tiles):
        r = lax.broadcasted_iota(jnp.int32, (rows_x, groups * 16), 0)
        c = lax.broadcasted_iota(jnp.int32, (rows_x, groups * 16), 1)
        pick.append(
            ((r // extra) * 16 + t * extra + r % extra == c).astype(F32).astype(BF16)
        )
    loads[1].wait()

    def use_chunk(k, carry):
        self_copy(k).wait()
        for d in range(1, groups):
            arrived(recv.at[k, ring(d)], recv_sem.at[k, ring(d)])
        rest = recv[k, :, tiles * MAIN :, :].reshape(groups * 16, WIDE)
        for t in range(tiles):
            at = slice(t * WIDE, (t + 1) * WIDE)
            lhs[0:rows_main, at] = recv[k, :, t * MAIN : (t + 1) * MAIN, :].reshape(
                rows_main, WIDE
            )
            lhs[rows_main:, at] = dot(pick[t], rest).astype(BF16)
        return carry

    def multiply(k, n):
        kat = pl.ds(pl.multiple_of(k * chunk, chunk), chunk)
        at = pl.ds(pl.multiple_of(n * block, block), block)
        new = acc[:, at] + lax.dot_general(
            lhs[...], w_v[at, kat], (((1,), (1,)), ((), ())), preferred_element_type=F32
        )
        acc[:, at] = new
        return new

    def whole_chunk(k, carry):
        use_chunk(k, carry)

        def tile(n, inner):
            multiply(k, n)
            return inner

        return lax.fori_loop(0, ff // block, tile, carry)

    lax.fori_loop(0, chunks - 1, whole_chunk, 0)
    c_sum[...] = jnp.zeros_like(c_sum)
    use_chunk(chunks - 1, 0)

    def last_tile(n, summed):
        new = multiply(chunks - 1, n)
        new = new * hid[:, pl.ds(pl.multiple_of(n * block, block), block)].astype(F32)
        for t in range(block // WIDE):
            summed = summed + new[:, t * WIDE : (t + 1) * WIDE]
        return summed

    summed = lax.fori_loop(0, ff // block, last_tile, jnp.zeros((rows_all, WIDE), F32))
    c_sum[0:rows_all] = summed
    c_send[...] = jnp.sum(jnp.transpose(c_sum[...]), axis=0, keepdims=True)
    c_recv[me] = c_send[...]

    def c_copy(d):
        return pltpu.make_async_remote_copy(
            src_ref=c_send,
            dst_ref=c_recv.at[me],
            send_sem=c_ss.at[d],
            recv_sem=c_rs.at[me],
            device_id=(q, ring(d)),
            device_id_type=MESH,
        )

    for d in order:
        c_copy(d).start()

    out_copies = []

    def finish(n):
        for first, factor, half in ((n * block, gfac, 0), (ff + n * block, ufac, 1)):
            back = acc[:, n * block : (n + 1) * block] * factor[:, n * block : (n + 1) * block]
            at = slice(first, first + block)
            out_v[:, at] = dot(to_natural, back.astype(BF16)).astype(BF16)
            one = pltpu.make_async_copy(out_v.at[:, at], out_hbm.at[:, at], out_sem.at[n, half])
            one.start()
            out_copies.append(one)

    parts = ff // block
    finish(0)

    for d in range(1, groups):
        arrived(c_recv.at[ring(d)], c_rs.at[ring(d)])
    c_wide = c_send.shape[-1]
    c_lane = lax.broadcasted_iota(jnp.int32, (tokens, c_wide), 1).astype(F32)
    me_f = me.astype(F32)
    prod = []
    for k in range(2):
        found = jnp.zeros((tokens, c_wide), F32)
        for e in range(groups):
            found = found + jnp.where(ident[k] == float(e), c_recv[e], 0.0)
        target = jnp.where(
            slot[k] < MAIN,
            me_f * MAIN + slot[k],
            rows_main + me_f * extra + slot[k] - MAIN,
        )
        prod.append(jnp.sum(jnp.where(c_lane == target, found, 0.0), axis=1, keepdims=True))
    mixture = weight[0] * prod[0] + weight[1] * prod[1]
    terms = jnp.zeros((tokens, WIDE), F32)
    for k in range(2):
        grad = (prod[k] - mixture) / total * score[k] * (1.0 - score[k])
        terms = terms + onehot[k] * grad
    terms = jnp.transpose(terms)[0:groups]
    high = terms.astype(BF16).astype(F32)
    middle = (terms - high).astype(BF16).astype(F32)
    low = terms - high - middle
    stack = jnp.concatenate([high, middle, low, jnp.zeros_like(low)], axis=0).astype(BF16)
    loads[2].wait()
    for n in range(chunks):
        at = slice(n * chunk, (n + 1) * chunk)
        three = dot(stack, x_v[:, at])
        part = three[0:groups] + three[groups : 2 * groups] + three[2 * groups : 3 * groups]
        for t in range(tiles):
            y_full[:, n * tiles + t, :] = part[:, t * WIDE : (t + 1) * WIDE]
    y_send[...] = y_full[...].astype(BF16)

    def y_copy(d):
        to = ring(d)
        return pltpu.make_async_remote_copy(
            src_ref=y_send.at[to],
            dst_ref=y_recv.at[me],
            send_sem=y_ss.at[d],
            recv_sem=y_rs.at[me],
            device_id=(q, to),
            device_id_type=MESH,
        )

    for d in order:
        y_copy(d).start()
    y_recv[me] = y_send[me]
    for n in range(1, max(parts - 1, 1)):
        finish(n)

    def sent(k, carry):
        for d in order:
            row_copy(k, d).wait_send()
        return carry

    for d in range(1, groups):
        arrived(y_recv.at[ring(d)], y_rs.at[ring(d)])

    def total_of(buffer, count):
        together = buffer[0].astype(F32)
        for j in range(1, count):
            together = together + buffer[j].astype(F32)
        return together

    g_send[...] = total_of(y_recv, groups).astype(BF16)

    def g_copy(d):
        to, _ = mate(d)
        return pltpu.make_async_remote_copy(
            src_ref=g_send,
            dst_ref=g_recv.at[rank],
            send_sem=g_ss.at[d],
            recv_sem=g_rs.at[rank],
            device_id=(to, me),
            device_id_type=MESH,
        )

    for d in sorted(range(1, team), key=lambda d: -min(d, team - d)):
        g_copy(d).start()
    g_recv[rank] = g_send[...]
    for n in range(max(parts - 1, 1), parts):
        finish(n)
    for d in range(1, team):
        arrived(g_recv.at[mate(d)[1]], g_rs.at[mate(d)[1]])

    z_send[...] = total_of(g_recv, team).astype(BF16)

    def z_copy(d):
        to, _ = zmate(d)
        return pltpu.make_async_remote_copy(
            src_ref=z_send,
            dst_ref=z_recv.at[zi],
            send_sem=z_ss.at[d],
            recv_sem=z_rs.at[zi],
            device_id=(to, me),
            device_id_type=MESH,
        )

    for d in sorted(range(1, nz), key=lambda d: -min(d, nz - d)):
        z_copy(d).start()
    z_recv[zi] = z_send[...]

    lax.fori_loop(0, chunks, sent, 0)
    for d in order:
        gate_copy(d).wait_send()
        c_copy(d).wait_send()
        y_copy(d).wait_send()
    for d in range(1, team):
        g_copy(d).wait_send()
    for one in out_copies:
        one.wait()

    for d in range(1, nz):
        arrived(z_recv.at[zmate(d)[1]], z_rs.at[zmate(d)[1]])
    row = total_of(z_recv, nz) * (1.0 / math.sqrt(tokens * nx * nz * nc * groups))
    for i in range(width // WIDE):
        router_ref[:, i * WIDE : (i + 1) * WIDE] = row[i : i + 1]
    for d in range(1, nz):
        z_copy(d).wait_send()


def body(dims, normed_input, output_grad, route_logits, route_ids, down_weight, pre_act):
    groups = lax.axis_size("expert")
    tokens, width = normed_input.shape
    ff = down_weight.shape[1]
    slots = pre_act.shape[0]
    cap = slots // groups
    nx, nz, nc = dims
    team = nx * nc
    extra = cap - MAIN
    tiles = 16 // extra
    chunk = tiles * WIDE
    chunks = width // chunk
    block_rows = tiles * MAIN + 16
    lines = -(-width // (16 * WIDE)) * 16
    c_wide = -(-slots // WIDE) * WIDE
    vmem = pl.BlockSpec(memory_space=pltpu.VMEM)
    anywhere = pl.BlockSpec(memory_space=pl.ANY)
    dma = pltpu.SemaphoreType.DMA
    grad, row = pl.pallas_call(
        functools.partial(kernel, dims, groups, cap),
        out_shape=(
            pltpu.VMEM((slots, 2 * ff), BF16),
            pltpu.VMEM((1, width), F32),
        ),
        in_specs=[anywhere] * 6,
        out_specs=(anywhere, vmem),
        scratch_shapes=[
            pltpu.VMEM(route_ids.shape[::-1], jnp.int32),
            pltpu.VMEM(route_logits.shape[::-1], F32),
            pltpu.VMEM((tokens, width), BF16),
            pltpu.VMEM((tokens, width), BF16),
            pltpu.VMEM((ff, width), BF16),
            pltpu.VMEM((slots, 2 * ff), BF16),
            pltpu.VMEM((chunks, groups, block_rows, WIDE), BF16),
            pltpu.VMEM((chunks, groups, block_rows, WIDE), BF16),
            pltpu.VMEM((slots, chunk), BF16),
            pltpu.VMEM((slots, ff), F32),
            pltpu.VMEM((slots, ff), BF16),
            pltpu.VMEM((slots, ff), F32),
            pltpu.VMEM((slots, ff), F32),
            pltpu.VMEM((slots, 2 * ff), BF16),
            pltpu.VMEM((groups, 1, WIDE), F32),
            pltpu.VMEM((groups, 1, WIDE), F32),
            pltpu.VMEM((c_wide, WIDE), F32),
            pltpu.VMEM((1, c_wide), F32),
            pltpu.VMEM((groups, 1, c_wide), F32),
            pltpu.VMEM((groups, lines, WIDE), F32),
            pltpu.VMEM((groups, lines, WIDE), BF16),
            pltpu.VMEM((groups, lines, WIDE), BF16),
            pltpu.VMEM((lines, WIDE), BF16),
            pltpu.VMEM((team, lines, WIDE), BF16),
            pltpu.VMEM((lines, WIDE), BF16),
            pltpu.VMEM((nz, lines, WIDE), BF16),
            dma((chunks,)),
            dma((5,)),
            dma((max(1, ff // 256), 2)),
            dma((chunks, groups)),
            dma((chunks, groups)),
            dma((chunks,)),
            dma((groups,)),
            dma((groups,)),
            dma((groups,)),
            dma((groups,)),
            dma((groups,)),
            dma((groups,)),
            dma((team,)),
            dma((team,)),
            dma((nz,)),
            dma((nz,)),
        ],
        compiler_params=pltpu.CompilerParams(
            collective_id=0, has_side_effects=True, vmem_limit_bytes=56 * 1024 * 1024
        ),
        cost_estimate=pl.CostEstimate(
            flops=2 * slots * width * ff, bytes_accessed=12 * 1024 * 1024, transcendentals=0
        ),
    )(route_ids.T, route_logits.T, normed_input, output_grad, down_weight, pre_act)
    return grad, row


def solution(mesh):
    dims = dp_dims(mesh.shape["dp"])
    return jax.shard_map(
        functools.partial(body, dims),
        mesh=mesh,
        in_specs=(
            P(("dp", "expert"), None),
            P(("dp", "expert"), None),
            P(("dp", "expert"), None),
            P(("dp", "expert"), None),
            P("expert", None, None),
            P(("dp", "expert"), None),
        ),
        out_specs=(P(("dp", "expert"), None), P("expert", None)),
        check_vma=False,
    )
```

```python
import functools
import math

import jax
import jax.numpy as jnp
from jax import lax
from jax.experimental import pallas as pl
from jax.experimental.pallas import tpu as pltpu
from jax.sharding import PartitionSpec as P

MESH = pl.DeviceIdType.MESH
F32 = jnp.float32
BF16 = jnp.bfloat16
MAIN = 32
WIDE = 128


def dot(a, b):
    return jnp.dot(a, b, preferred_element_type=F32)


def dp_dims(n_dp):
    return (4, n_dp // 8, 2)


def kernel(
    dims,
    groups,
    cap,
    ids_hbm,
    logits_hbm,
    x_hbm,
    g_hbm,
    w_hbm,
    pre_hbm,
    out_ref,
    router_ref,
    ids_ref,
    logits_ref,
    g_v,
    x_v,
    w_v,
    pre_v,
    send,
    recv,
    lhs,
    acc,
    hid,
    gfac,
    ufac,
    ahead,
    ahead_extra,
    masks,
    gate_send,
    gate_recv,
    c_sum,
    c_send,
    c_recv,
    y_full,
    y_send,
    y_recv,
    g_send,
    g_recv,
    z_send,
    z_recv,
    g_sem,
    load_sem,
    send_sem,
    recv_sem,
    self_sem,
    gate_ss,
    gate_rs,
    c_ss,
    c_rs,
    y_ss,
    y_rs,
    g_ss,
    g_rs,
    z_ss,
    z_rs,
):
    nx, nz, nc = dims
    team = nx * nc
    tokens, width = g_v.shape
    ff = w_v.shape[0]
    extra = cap - MAIN
    tiles = 16 // extra
    chunk = tiles * WIDE
    chunks = width // chunk
    rows_main = groups * MAIN
    rows_all = groups * cap

    q = lax.axis_index("dp")
    me = lax.axis_index("expert")
    core = lax.rem(q, nc)
    zi = lax.rem(q // nc, nz)
    xi = q // (nc * nz)
    rank = xi * nc + core

    def ring(d):
        return lax.rem(me + d, groups)

    def mate(d):
        r = lax.rem(rank + d, team)
        return ((r // nc) * nz + zi) * nc + lax.rem(r, nc), r

    def zmate(d):
        z = lax.rem(zi + d, nz)
        return (xi * nz + z) * nc + core, z

    ids_load = pltpu.make_async_copy(ids_hbm, ids_ref, load_sem.at[3])
    logits_load = pltpu.make_async_copy(logits_hbm, logits_ref, load_sem.at[4])
    ids_load.start()
    g_loads = [
        pltpu.make_async_copy(
            g_hbm.at[:, k * chunk : (k + 1) * chunk],
            g_v.at[:, k * chunk : (k + 1) * chunk],
            g_sem.at[k],
        )
        for k in range(chunks)
    ]
    for one in g_loads:
        one.start()
    logits_load.start()

    barrier = pltpu.get_barrier_semaphore()
    for d in range(1, groups):
        pl.semaphore_signal(barrier, inc=1, device_id=(q, ring(d)), device_id_type=MESH)
    for d in range(1, team):
        pl.semaphore_signal(barrier, inc=1, device_id=(mate(d)[0], me), device_id_type=MESH)
    for d in range(1, nz):
        pl.semaphore_signal(barrier, inc=1, device_id=(zmate(d)[0], me), device_id_type=MESH)

    loads = [
        pltpu.make_async_copy(pre_hbm, pre_v, load_sem.at[0]),
        pltpu.make_async_copy(w_hbm.at[0], w_v, load_sem.at[1]),
        pltpu.make_async_copy(x_hbm, x_v, load_sem.at[2]),
    ]

    ids_load.wait()
    ids = ids_ref[...].astype(F32)
    expert = lax.broadcasted_iota(jnp.int32, (16, tokens), 0).astype(F32)
    onehot_t = [(ids[k : k + 1] == expert).astype(F32) for k in range(2)]
    before = (
        lax.broadcasted_iota(jnp.int32, (tokens, tokens), 0)
        < lax.broadcasted_iota(jnp.int32, (tokens, tokens), 1)
    ).astype(F32)
    count_t = dot((onehot_t[0] + onehot_t[1]).astype(BF16), before.astype(BF16))
    slot_t = [jnp.sum(o * count_t, axis=0, keepdims=True) for o in onehot_t]
    to_main, to_extra = [], []
    for k in range(2):
        inside = slot_t[k] < MAIN
        at_k = ids[k : k + 1]
        to_main.append(jnp.where(inside, at_k * MAIN + slot_t[k], -1.0))
        to_extra.append(jnp.where(inside, -1000.0, at_k * 16 + slot_t[k] - MAIN))
    row_main = lax.broadcasted_iota(jnp.int32, (rows_main, tokens), 0).astype(F32)
    row_extra = lax.broadcasted_iota(jnp.int32, (groups * 16, tokens), 0).astype(F32)
    place_main = (
        (row_main == to_main[0]).astype(F32) + (row_main == to_main[1]).astype(F32)
    ).astype(BF16)
    place_extra = [
        (
            (row_extra == to_extra[0] + extra * t).astype(F32)
            + (row_extra == to_extra[1] + extra * t).astype(F32)
        ).astype(BF16)
        for t in range(tiles)
    ]

    order = sorted(range(1, groups), key=lambda d: -min(d, groups - d))

    def gate_copy(d):
        to = ring(d)
        return pltpu.make_async_remote_copy(
            src_ref=gate_send.at[to],
            dst_ref=gate_recv.at[me],
            send_sem=gate_ss.at[d],
            recv_sem=gate_rs.at[me],
            device_id=(q, to),
            device_id_type=MESH,
        )

    def row_copy(k, d):
        to = ring(d)
        return pltpu.make_async_remote_copy(
            src_ref=send.at[k, to],
            dst_ref=recv.at[k, me],
            send_sem=send_sem.at[k, d],
            recv_sem=recv_sem.at[k, me],
            device_id=(q, to),
            device_id_type=MESH,
        )

    def self_copy(k):
        return pltpu.make_async_copy(send.at[k, me], recv.at[k, me], self_sem.at[k])

    def arrived(buffer, sem):
        pltpu.make_async_copy(buffer, buffer, sem).wait()

    def fill_chunk(k):
        cols = g_v[:, pl.ds(pl.multiple_of(k * chunk, chunk), chunk)]
        main = dot(place_main, cols).astype(BF16)
        rest = jnp.zeros((groups * 16, WIDE), F32)
        for t in range(tiles):
            piece_t = main[:, t * WIDE : (t + 1) * WIDE]
            send[k, :, t * MAIN : (t + 1) * MAIN, :] = piece_t.reshape(groups, MAIN, WIDE)
            rest = rest + dot(place_extra[t], cols[:, t * WIDE : (t + 1) * WIDE])
        send[k, :, tiles * MAIN :, :] = rest.astype(BF16).reshape(groups, 16, WIDE)

    def start_chunk(k):
        for d in order:
            row_copy(k, d).start()
        self_copy(k).start()

    g_loads[0].wait()
    fill_chunk(0)
    pl.semaphore_wait(barrier, groups - 1 + team - 1 + nz - 1)
    start_chunk(0)
    for one in loads:
        one.start()

    logits_load.wait()
    scores_t = jax.nn.sigmoid(logits_ref[...])
    score_t = [scores_t[k : k + 1] for k in range(2)]
    total_t = score_t[0] + score_t[1]
    weight_t = [v / total_t for v in score_t]
    slot_row = lax.broadcasted_iota(jnp.int32, (WIDE, tokens), 0).astype(F32)
    gates = jnp.zeros((16, WIDE), F32)
    for k in range(2):
        gate = weight_t[k].astype(BF16).astype(F32)
        gates = gates + lax.dot_general(
            (onehot_t[k] * gate).astype(BF16),
            (slot_row == slot_t[k]).astype(F32).astype(BF16),
            (((1,), (1,)), ((), ())),
            preferred_element_type=F32,
        )
    for e in range(groups):
        gate_send[e] = gates[e : e + 1]
    for d in order:
        gate_copy(d).start()
    gate_recv[me] = gate_send[me]

    def send_chunk(k, carry):
        at = pl.ds(pl.multiple_of(k * chunk, chunk), chunk)
        pltpu.make_async_copy(g_hbm.at[:, at], g_v.at[:, at], g_sem.at[k]).wait()
        fill_chunk(k)
        start_chunk(k)
        return carry

    lax.fori_loop(1, chunks, send_chunk, 0)

    rows = [ids[0:1], ids[1:2], *slot_t, *score_t, *weight_t, total_t]
    rows.append(jnp.zeros((WIDE - len(rows), tokens), F32))
    columns = jnp.transpose(jnp.concatenate(rows, axis=0))
    column = [columns[:, i : i + 1] for i in range(9)]
    ident, slot, score, weight, total = (
        column[0:2],
        column[2:4],
        column[4:6],
        column[6:8],
        column[8],
    )
    lane = lax.broadcasted_iota(jnp.int32, (tokens, WIDE), 1).astype(F32)
    onehot = [(i == lane).astype(F32) for i in ident]
    y_full[...] = jnp.zeros_like(y_full)

    for d in range(1, groups):
        arrived(gate_recv.at[ring(d)], gate_rs.at[ring(d)])
    lane_m = lax.broadcasted_iota(jnp.int32, (MAIN, WIDE), 1)
    row_m = lax.broadcasted_iota(jnp.int32, (MAIN, WIDE), 0)
    rows_x = rows_all - rows_main
    lane_x = lax.broadcasted_iota(jnp.int32, (rows_x, WIDE), 1)
    row_x = lax.broadcasted_iota(jnp.int32, (rows_x, WIDE), 0)
    gate_x = jnp.zeros((rows_x, WIDE), F32)
    gate_parts = []
    for j in range(groups):
        one = gate_recv[j]
        gate_parts.append(
            jnp.sum(jnp.where(lane_m == row_m, one, 0.0), axis=1, keepdims=True)
        )
        mine = (row_x // extra == j) & (lane_x == MAIN + row_x % extra)
        gate_x = gate_x + jnp.where(mine, one, 0.0)
    gate_parts.append(jnp.sum(gate_x, axis=1, keepdims=True))
    gate_col = jnp.concatenate(gate_parts, axis=0)

    def natural(r):
        s = r - rows_main
        return jnp.where(
            r < rows_main,
            (r // MAIN) * cap + r % MAIN,
            (s // extra) * cap + MAIN + s % extra,
        )

    square_r = lax.broadcasted_iota(jnp.int32, (rows_all, rows_all), 0)
    square_c = lax.broadcasted_iota(jnp.int32, (rows_all, rows_all), 1)
    to_mine = (natural(square_r) == square_c).astype(F32).astype(BF16)
    to_natural = (natural(square_c) == square_r).astype(F32).astype(BF16)
    loads[0].wait()
    block = 256

    def prepare(n, carry):
        at = pl.ds(pl.multiple_of(n * block, block), block)
        at_up = pl.ds(pl.multiple_of(ff + n * block, block), block)
        g = dot(to_mine, pre_v[:, at])
        u = dot(to_mine, pre_v[:, at_up])
        s = jax.nn.sigmoid(g)
        gs = g * s
        hid[:, at] = (gs * u).astype(BF16)
        gfac[:, at] = gate_col * u * s * (1.0 + g * (1.0 - s))
        ufac[:, at] = gate_col * gs
        return carry

    lax.fori_loop(0, ff // block, prepare, 0)
    acc[...] = jnp.zeros_like(acc)
    pick = []
    for t in range(tiles):
        r = lax.broadcasted_iota(jnp.int32, (rows_x, groups * 16), 0)
        c = lax.broadcasted_iota(jnp.int32, (rows_x, groups * 16), 1)
        pick.append(
            ((r // extra) * 16 + t * extra + r % extra == c).astype(F32).astype(BF16)
        )
    loads[1].wait()

    final = chunks - 1

    def work_ahead(n, carry):
        at = pl.ds(pl.multiple_of(n * block, block), block)
        w_at = pl.ds(pl.multiple_of(final * chunk + n * block, block), block)
        ahead[:, at] = dot(hid[...], w_v[:, w_at]).astype(BF16)
        return carry

    lax.fori_loop(0, chunk // block, work_ahead, 0)
    packed_extra = jnp.zeros((groups * 16, WIDE), F32)
    for t in range(tiles):
        packed_extra = packed_extra + lax.dot_general(
            pick[t],
            ahead[rows_main:, t * WIDE : (t + 1) * WIDE],
            (((0,), (0,)), ((), ())),
            preferred_element_type=F32,
        )
    ahead_extra[...] = packed_extra.astype(BF16)

    c_wide = c_send.shape[-1]
    c_lane = lax.broadcasted_iota(jnp.int32, (tokens, c_wide), 1)
    c_mod = (c_lane % extra).astype(F32)
    in_extra = (c_lane >= rows_main + me * 16) & (c_lane < rows_main + me * 16 + 16)
    last_at = rows_main + groups * 16 + me * extra
    in_extra = in_extra | ((c_lane >= last_at) & (c_lane < last_at + extra))
    c_lane = c_lane.astype(F32)
    me_f = me.astype(F32)
    for k in range(2):
        hit = jnp.where(c_lane == me_f * MAIN + slot[k], 1.0, 0.0)
        over = jnp.where(in_extra & (c_mod == slot[k] - MAIN), 1.0, 0.0)
        masks[k] = jnp.where(slot[k] < MAIN, hit, over)

    def wait_chunk(k):
        self_copy(k).wait()
        for d in range(1, groups):
            arrived(recv.at[k, ring(d)], recv_sem.at[k, ring(d)])

    def use_chunk(k, carry):
        rest = recv[k, :, tiles * MAIN :, :].reshape(groups * 16, WIDE)
        for t in range(tiles):
            at = slice(t * WIDE, (t + 1) * WIDE)
            lhs[0:rows_main, at] = recv[k, :, t * MAIN : (t + 1) * MAIN, :].reshape(
                rows_main, WIDE
            )
            lhs[rows_main:, at] = dot(pick[t], rest).astype(BF16)
        return carry

    def multiply(k, n):
        kat = pl.ds(pl.multiple_of(k * chunk, chunk), chunk)
        at = pl.ds(pl.multiple_of(n * block, block), block)
        new = acc[:, at] + lax.dot_general(
            lhs[...], w_v[at, kat], (((1,), (1,)), ((), ())), preferred_element_type=F32
        )
        acc[:, at] = new
        return new

    def whole_chunk(k, carry):
        wait_chunk(k)
        use_chunk(k, carry)

        def tile(n, inner):
            multiply(k, n)
            return inner

        return lax.fori_loop(0, ff // block, tile, carry)

    lax.fori_loop(0, chunks - 1, whole_chunk, 0)
    c_sum[...] = jnp.zeros_like(c_sum)

    summed = jnp.zeros((rows_all, WIDE), F32)
    for n in range(ff // WIDE):
        at = slice(n * WIDE, (n + 1) * WIDE)
        summed = summed + hid[:, at].astype(F32) * acc[:, at]
    first_extra = rows_main + groups * 16
    c_sum[0:rows_main] = summed[0:rows_main]
    c_sum[first_extra : first_extra + rows_x] = summed[rows_main:]
    wait_chunk(final)
    summed = c_sum[0:rows_main]
    for t in range(tiles):
        come = recv[final, :, t * MAIN : (t + 1) * MAIN, :].reshape(rows_main, WIDE)
        held = ahead[0:rows_main, t * WIDE : (t + 1) * WIDE]
        summed = summed + come.astype(F32) * held.astype(F32)
    c_sum[0:rows_main] = summed
    come = recv[final, :, tiles * MAIN :, :].reshape(groups * 16, WIDE)
    c_sum[rows_main:first_extra] = come.astype(F32) * ahead_extra[...].astype(F32)
    c_send[...] = jnp.sum(jnp.transpose(c_sum[...]), axis=0, keepdims=True)
    c_recv[me] = c_send[...]

    def c_copy(d):
        return pltpu.make_async_remote_copy(
            src_ref=c_send,
            dst_ref=c_recv.at[me],
            send_sem=c_ss.at[d],
            recv_sem=c_rs.at[me],
            device_id=(q, ring(d)),
            device_id_type=MESH,
        )

    for d in order:
        c_copy(d).start()

    use_chunk(final, 0)

    def last_tile(n, carry):
        multiply(final, n)
        return carry

    lax.fori_loop(0, ff // block, last_tile, 0)

    def finish(n):
        for first, factor in ((n * block, gfac), (ff + n * block, ufac)):
            back = acc[:, n * block : (n + 1) * block] * factor[:, n * block : (n + 1) * block]
            out_ref[:, first : first + block] = dot(to_natural, back.astype(BF16)).astype(BF16)

    parts = ff // block
    turns = [list(range(parts))[i::3] for i in range(3)]

    for d in range(1, groups):
        arrived(c_recv.at[ring(d)], c_rs.at[ring(d)])
    prod = []
    for k in range(2):
        found = jnp.zeros((tokens, c_wide), F32)
        for e in range(groups):
            found = found + jnp.where(ident[k] == float(e), c_recv[e], 0.0)
        prod.append(jnp.sum(found * masks[k], axis=1, keepdims=True))
    mixture = weight[0] * prod[0] + weight[1] * prod[1]
    terms = jnp.zeros((tokens, WIDE), F32)
    for k in range(2):
        grad = (prod[k] - mixture) / total * score[k] * (1.0 - score[k])
        terms = terms + onehot[k] * grad
    terms = jnp.transpose(terms)[0:groups]
    high = terms.astype(BF16).astype(F32)
    middle = (terms - high).astype(BF16).astype(F32)
    low = terms - high - middle
    stack = jnp.concatenate([high, middle, low, jnp.zeros_like(low)], axis=0).astype(BF16)
    loads[2].wait()
    for n in range(chunks):
        at = slice(n * chunk, (n + 1) * chunk)
        three = dot(stack, x_v[:, at])
        part = three[0:groups] + three[groups : 2 * groups] + three[2 * groups : 3 * groups]
        for t in range(tiles):
            y_full[:, n * tiles + t, :] = part[:, t * WIDE : (t + 1) * WIDE]
    y_send[...] = y_full[...].astype(BF16)

    def y_copy(d):
        to = ring(d)
        return pltpu.make_async_remote_copy(
            src_ref=y_send.at[to],
            dst_ref=y_recv.at[me],
            send_sem=y_ss.at[d],
            recv_sem=y_rs.at[me],
            device_id=(q, to),
            device_id_type=MESH,
        )

    for d in order:
        y_copy(d).start()
    y_recv[me] = y_send[me]
    for n in turns[0]:
        finish(n)

    def sent(k, carry):
        for d in order:
            row_copy(k, d).wait_send()
        return carry

    for d in range(1, groups):
        arrived(y_recv.at[ring(d)], y_rs.at[ring(d)])

    def total_of(buffer, count):
        together = buffer[0].astype(F32)
        for j in range(1, count):
            together = together + buffer[j].astype(F32)
        return together

    g_send[...] = total_of(y_recv, groups).astype(BF16)

    def g_copy(d):
        to, _ = mate(d)
        return pltpu.make_async_remote_copy(
            src_ref=g_send,
            dst_ref=g_recv.at[rank],
            send_sem=g_ss.at[d],
            recv_sem=g_rs.at[rank],
            device_id=(to, me),
            device_id_type=MESH,
        )

    for d in sorted(range(1, team), key=lambda d: -min(d, team - d)):
        g_copy(d).start()
    g_recv[rank] = g_send[...]
    for n in turns[1]:
        finish(n)
    for d in range(1, team):
        arrived(g_recv.at[mate(d)[1]], g_rs.at[mate(d)[1]])

    z_send[...] = total_of(g_recv, team).astype(BF16)

    def z_copy(d):
        to, _ = zmate(d)
        return pltpu.make_async_remote_copy(
            src_ref=z_send,
            dst_ref=z_recv.at[zi],
            send_sem=z_ss.at[d],
            recv_sem=z_rs.at[zi],
            device_id=(to, me),
            device_id_type=MESH,
        )

    for d in sorted(range(1, nz), key=lambda d: -min(d, nz - d)):
        z_copy(d).start()
    z_recv[zi] = z_send[...]

    lax.fori_loop(0, chunks, sent, 0)
    for d in order:
        gate_copy(d).wait_send()
        c_copy(d).wait_send()
        y_copy(d).wait_send()
    for d in range(1, team):
        g_copy(d).wait_send()
    for n in turns[2]:
        finish(n)

    for d in range(1, nz):
        arrived(z_recv.at[zmate(d)[1]], z_rs.at[zmate(d)[1]])
    row = total_of(z_recv, nz) * (1.0 / math.sqrt(tokens * nx * nz * nc * groups))
    for i in range(width // WIDE):
        router_ref[:, i * WIDE : (i + 1) * WIDE] = row[i : i + 1]
    for d in range(1, nz):
        z_copy(d).wait_send()


def hand_out(grad_in, row_in, grad_out, row_out, sem):
    rows = grad_in.shape[0]
    step = 96 if rows % 96 == 0 else rows
    copies = [pltpu.make_async_copy(row_in, row_out, sem.at[0])]
    for i in range(rows // step):
        at = slice(i * step, (i + 1) * step)
        copies.append(pltpu.make_async_copy(grad_in.at[at], grad_out.at[at], sem.at[i + 1]))
    for one in copies:
        one.start()
    for one in copies:
        one.wait()


def body(dims, normed_input, output_grad, route_logits, route_ids, down_weight, pre_act):
    groups = lax.axis_size("expert")
    tokens, width = normed_input.shape
    ff = down_weight.shape[1]
    slots = pre_act.shape[0]
    cap = slots // groups
    nx, nz, nc = dims
    team = nx * nc
    extra = cap - MAIN
    tiles = 16 // extra
    chunk = tiles * WIDE
    chunks = width // chunk
    block_rows = tiles * MAIN + 16
    lines = -(-width // (16 * WIDE)) * 16
    c_wide = groups * (MAIN + 16) + -(-groups * extra // WIDE) * WIDE
    vmem = pl.BlockSpec(memory_space=pltpu.VMEM)
    anywhere = pl.BlockSpec(memory_space=pl.ANY)
    dma = pltpu.SemaphoreType.DMA
    grad, row = pl.pallas_call(
        functools.partial(kernel, dims, groups, cap),
        out_shape=(
            pltpu.VMEM((slots, 2 * ff), BF16),
            pltpu.VMEM((1, width), F32),
        ),
        in_specs=[anywhere] * 6,
        out_specs=(vmem, vmem),
        scratch_shapes=[
            pltpu.VMEM(route_ids.shape[::-1], jnp.int32),
            pltpu.VMEM(route_logits.shape[::-1], F32),
            pltpu.VMEM((tokens, width), BF16),
            pltpu.VMEM((tokens, width), BF16),
            pltpu.VMEM((ff, width), BF16),
            pltpu.VMEM((slots, 2 * ff), BF16),
            pltpu.VMEM((chunks, groups, block_rows, WIDE), BF16),
            pltpu.VMEM((chunks, groups, block_rows, WIDE), BF16),
            pltpu.VMEM((slots, chunk), BF16),
            pltpu.VMEM((slots, ff), F32),
            pltpu.VMEM((slots, ff), BF16),
            pltpu.VMEM((slots, ff), F32),
            pltpu.VMEM((slots, ff), F32),
            pltpu.VMEM((slots, chunk), BF16),
            pltpu.VMEM((groups * 16, WIDE), BF16),
            pltpu.VMEM((2, tokens, c_wide), F32),
            pltpu.VMEM((groups, 1, WIDE), F32),
            pltpu.VMEM((groups, 1, WIDE), F32),
            pltpu.VMEM((c_wide, WIDE), F32),
            pltpu.VMEM((1, c_wide), F32),
            pltpu.VMEM((groups, 1, c_wide), F32),
            pltpu.VMEM((groups, lines, WIDE), F32),
            pltpu.VMEM((groups, lines, WIDE), BF16),
            pltpu.VMEM((groups, lines, WIDE), BF16),
            pltpu.VMEM((lines, WIDE), BF16),
            pltpu.VMEM((team, lines, WIDE), BF16),
            pltpu.VMEM((lines, WIDE), BF16),
            pltpu.VMEM((nz, lines, WIDE), BF16),
            dma((chunks,)),
            dma((5,)),
            dma((chunks, groups)),
            dma((chunks, groups)),
            dma((chunks,)),
            dma((groups,)),
            dma((groups,)),
            dma((groups,)),
            dma((groups,)),
            dma((groups,)),
            dma((groups,)),
            dma((team,)),
            dma((team,)),
            dma((nz,)),
            dma((nz,)),
        ],
        compiler_params=pltpu.CompilerParams(
            collective_id=0, has_side_effects=True, vmem_limit_bytes=56 * 1024 * 1024
        ),
        cost_estimate=pl.CostEstimate(
            flops=2 * slots * width * ff, bytes_accessed=12 * 1024 * 1024, transcendentals=0
        ),
    )(route_ids.T, route_logits.T, normed_input, output_grad, down_weight, pre_act)
    return pl.pallas_call(
        hand_out,
        out_shape=(
            jax.ShapeDtypeStruct(grad.shape, grad.dtype),
            jax.ShapeDtypeStruct(row.shape, row.dtype),
        ),
        in_specs=[vmem, vmem],
        out_specs=(anywhere, anywhere),
        scratch_shapes=[
            dma((8,)),
        ],
        cost_estimate=pl.CostEstimate(
            flops=0, bytes_accessed=4 * slots * ff * 2, transcendentals=0
        ),
    )(
        pltpu.with_memory_space_constraint(grad, pltpu.VMEM),
        pltpu.with_memory_space_constraint(row, pltpu.VMEM),
    )


def solution(mesh):
    dims = dp_dims(mesh.shape["dp"])
    return jax.shard_map(
        functools.partial(body, dims),
        mesh=mesh,
        in_specs=(
            P(("dp", "expert"), None),
            P(("dp", "expert"), None),
            P(("dp", "expert"), None),
            P(("dp", "expert"), None),
            P("expert", None, None),
            P(("dp", "expert"), None),
        ),
        out_specs=(P(("dp", "expert"), None), P("expert", None)),
        check_vma=False,
    )
```

```python
import functools
import math

import jax
import jax.numpy as jnp
from jax import lax
from jax.experimental import pallas as pl
from jax.experimental.pallas import tpu as pltpu
from jax.sharding import PartitionSpec as P

MESH = pl.DeviceIdType.MESH
F32 = jnp.float32
BF16 = jnp.bfloat16
MAIN = 32
WIDE = 128


def dot(a, b):
    return jnp.dot(a, b, preferred_element_type=F32)


def dp_dims(n_dp):
    return (4, n_dp // 8, 2)


def kernel(
    dims,
    groups,
    cap,
    ids_hbm,
    logits_hbm,
    x_hbm,
    g_hbm,
    w_hbm,
    pre_hbm,
    out_ref,
    router_ref,
    ids_ref,
    logits_ref,
    g_v,
    x_v,
    w_v,
    pre_v,
    send,
    recv,
    lhs,
    acc,
    hid,
    gfac,
    ufac,
    ahead,
    ahead_extra,
    masks,
    gate_send,
    gate_recv,
    c_sum,
    c_send,
    c_recv,
    y_full,
    y_send,
    y_recv,
    g_send,
    g_recv,
    z_send,
    z_recv,
    g_sem,
    load_sem,
    send_sem,
    recv_sem,
    self_sem,
    gate_ss,
    gate_rs,
    c_ss,
    c_rs,
    y_ss,
    y_rs,
    g_ss,
    g_rs,
    z_ss,
    z_rs,
):
    nx, nz, nc = dims
    team = nx * nc
    tokens, width = g_v.shape
    ff = w_v.shape[0]
    extra = cap - MAIN
    tiles = 16 // extra
    chunk = tiles * WIDE
    chunks = width // chunk
    rows_main = groups * MAIN
    rows_all = groups * cap

    q = lax.axis_index("dp")
    me = lax.axis_index("expert")
    core = lax.rem(q, nc)
    zi = lax.rem(q // nc, nz)
    xi = q // (nc * nz)
    rank = xi * nc + core

    def ring(d):
        return lax.rem(me + d, groups)

    def mate(d):
        r = lax.rem(rank + d, team)
        return ((r // nc) * nz + zi) * nc + lax.rem(r, nc), r

    def zmate(d):
        z = lax.rem(zi + d, nz)
        return (xi * nz + z) * nc + core, z

    ids_load = pltpu.make_async_copy(ids_hbm, ids_ref, load_sem.at[3])
    logits_load = pltpu.make_async_copy(logits_hbm, logits_ref, load_sem.at[4])
    ids_load.start()
    barrier = pltpu.get_barrier_semaphore()
    near_last = sorted(range(1, groups), key=lambda d: -min(d, groups - d))
    for d in near_last:
        pl.semaphore_signal(barrier, inc=1, device_id=(q, ring(d)), device_id_type=MESH)
    g_loads = [
        pltpu.make_async_copy(
            g_hbm.at[:, k * chunk : (k + 1) * chunk],
            g_v.at[:, k * chunk : (k + 1) * chunk],
            g_sem.at[k],
        )
        for k in range(chunks)
    ]
    for one in g_loads:
        one.start()
    for d in range(1, team):
        pl.semaphore_signal(barrier, inc=1, device_id=(mate(d)[0], me), device_id_type=MESH)
    for d in sorted(range(1, nz), key=lambda d: -min(d, nz - d)):
        pl.semaphore_signal(barrier, inc=1, device_id=(zmate(d)[0], me), device_id_type=MESH)

    logits_load.start()

    loads = [
        pltpu.make_async_copy(pre_hbm, pre_v, load_sem.at[0]),
        pltpu.make_async_copy(w_hbm.at[0], w_v, load_sem.at[1]),
        pltpu.make_async_copy(x_hbm, x_v, load_sem.at[2]),
    ]

    ids_load.wait()
    ids = ids_ref[...].astype(F32)
    expert = lax.broadcasted_iota(jnp.int32, (16, tokens), 0).astype(F32)
    onehot_t = [(ids[k : k + 1] == expert).astype(F32) for k in range(2)]
    before = (
        lax.broadcasted_iota(jnp.int32, (tokens, tokens), 0)
        < lax.broadcasted_iota(jnp.int32, (tokens, tokens), 1)
    ).astype(F32)
    count_t = dot((onehot_t[0] + onehot_t[1]).astype(BF16), before.astype(BF16))
    slot_t = [jnp.sum(o * count_t, axis=0, keepdims=True) for o in onehot_t]
    to_main, to_extra = [], []
    for k in range(2):
        inside = slot_t[k] < MAIN
        at_k = ids[k : k + 1]
        to_main.append(jnp.where(inside, at_k * MAIN + slot_t[k], -1.0))
        to_extra.append(jnp.where(inside, -1000.0, at_k * 16 + slot_t[k] - MAIN))
    row_main = lax.broadcasted_iota(jnp.int32, (rows_main, tokens), 0).astype(F32)
    row_extra = lax.broadcasted_iota(jnp.int32, (groups * 16, tokens), 0).astype(F32)
    place_main = (
        (row_main == to_main[0]).astype(F32) + (row_main == to_main[1]).astype(F32)
    ).astype(BF16)
    place_extra = [
        (
            (row_extra == to_extra[0] + extra * t).astype(F32)
            + (row_extra == to_extra[1] + extra * t).astype(F32)
        ).astype(BF16)
        for t in range(tiles)
    ]

    order = near_last

    def gate_copy(d):
        to = ring(d)
        return pltpu.make_async_remote_copy(
            src_ref=gate_send.at[to],
            dst_ref=gate_recv.at[me],
            send_sem=gate_ss.at[d],
            recv_sem=gate_rs.at[me],
            device_id=(q, to),
            device_id_type=MESH,
        )

    def row_copy(k, d):
        to = ring(d)
        return pltpu.make_async_remote_copy(
            src_ref=send.at[k, to],
            dst_ref=recv.at[k, me],
            send_sem=send_sem.at[k, d],
            recv_sem=recv_sem.at[k, me],
            device_id=(q, to),
            device_id_type=MESH,
        )

    def self_copy(k):
        return pltpu.make_async_copy(send.at[k, me], recv.at[k, me], self_sem.at[k])

    def arrived(buffer, sem):
        pltpu.make_async_copy(buffer, buffer, sem).wait()

    def fill_chunk(k):
        cols = g_v[:, pl.ds(pl.multiple_of(k * chunk, chunk), chunk)]
        main = dot(place_main, cols).astype(BF16)
        rest = jnp.zeros((groups * 16, WIDE), F32)
        for t in range(tiles):
            piece_t = main[:, t * WIDE : (t + 1) * WIDE]
            send[k, :, t * MAIN : (t + 1) * MAIN, :] = piece_t.reshape(groups, MAIN, WIDE)
            rest = rest + dot(place_extra[t], cols[:, t * WIDE : (t + 1) * WIDE])
        send[k, :, tiles * MAIN :, :] = rest.astype(BF16).reshape(groups, 16, WIDE)

    def start_chunk(k):
        for d in order:
            row_copy(k, d).start()
        self_copy(k).start()

    g_loads[0].wait()
    fill_chunk(0)
    pl.semaphore_wait(barrier, groups - 1 + team - 1 + nz - 1)
    start_chunk(0)
    for one in loads:
        one.start()

    logits_load.wait()
    scores_t = jax.nn.sigmoid(logits_ref[...])
    score_t = [scores_t[k : k + 1] for k in range(2)]
    total_t = score_t[0] + score_t[1]
    weight_t = [v / total_t for v in score_t]
    slot_row = lax.broadcasted_iota(jnp.int32, (WIDE, tokens), 0).astype(F32)
    gates = jnp.zeros((16, WIDE), F32)
    for k in range(2):
        gate = weight_t[k].astype(BF16).astype(F32)
        gates = gates + lax.dot_general(
            (onehot_t[k] * gate).astype(BF16),
            (slot_row == slot_t[k]).astype(F32).astype(BF16),
            (((1,), (1,)), ((), ())),
            preferred_element_type=F32,
        )
    for e in range(groups):
        gate_send[e] = gates[e : e + 1]
    for d in order:
        gate_copy(d).start()
    gate_recv[me] = gate_send[me]

    def send_chunk(k, carry):
        at = pl.ds(pl.multiple_of(k * chunk, chunk), chunk)
        pltpu.make_async_copy(g_hbm.at[:, at], g_v.at[:, at], g_sem.at[k]).wait()
        fill_chunk(k)
        start_chunk(k)
        return carry

    lax.fori_loop(1, chunks, send_chunk, 0)

    rows = [ids[0:1], ids[1:2], *slot_t, *score_t, *weight_t, total_t]
    rows.append(jnp.zeros((WIDE - len(rows), tokens), F32))
    columns = jnp.transpose(jnp.concatenate(rows, axis=0))
    column = [columns[:, i : i + 1] for i in range(9)]
    ident, slot, score, weight, total = (
        column[0:2],
        column[2:4],
        column[4:6],
        column[6:8],
        column[8],
    )
    lane = lax.broadcasted_iota(jnp.int32, (tokens, WIDE), 1).astype(F32)
    onehot = [(i == lane).astype(F32) for i in ident]
    y_full[...] = jnp.zeros_like(y_full)

    for d in range(1, groups):
        arrived(gate_recv.at[ring(d)], gate_rs.at[ring(d)])
    lane_m = lax.broadcasted_iota(jnp.int32, (MAIN, WIDE), 1)
    row_m = lax.broadcasted_iota(jnp.int32, (MAIN, WIDE), 0)
    rows_x = rows_all - rows_main
    lane_x = lax.broadcasted_iota(jnp.int32, (rows_x, WIDE), 1)
    row_x = lax.broadcasted_iota(jnp.int32, (rows_x, WIDE), 0)
    gate_x = jnp.zeros((rows_x, WIDE), F32)
    gate_parts = []
    for j in range(groups):
        one = gate_recv[j]
        gate_parts.append(
            jnp.sum(jnp.where(lane_m == row_m, one, 0.0), axis=1, keepdims=True)
        )
        mine = (row_x // extra == j) & (lane_x == MAIN + row_x % extra)
        gate_x = gate_x + jnp.where(mine, one, 0.0)
    gate_parts.append(jnp.sum(gate_x, axis=1, keepdims=True))
    gate_col = jnp.concatenate(gate_parts, axis=0)

    def natural(r):
        s = r - rows_main
        return jnp.where(
            r < rows_main,
            (r // MAIN) * cap + r % MAIN,
            (s // extra) * cap + MAIN + s % extra,
        )

    square_r = lax.broadcasted_iota(jnp.int32, (rows_all, rows_all), 0)
    square_c = lax.broadcasted_iota(jnp.int32, (rows_all, rows_all), 1)
    to_mine = (natural(square_r) == square_c).astype(F32).astype(BF16)
    to_natural = (natural(square_c) == square_r).astype(F32).astype(BF16)
    loads[0].wait()
    block = 256

    def prepare(n, carry):
        at = pl.ds(pl.multiple_of(n * block, block), block)
        at_up = pl.ds(pl.multiple_of(ff + n * block, block), block)
        g = dot(to_mine, pre_v[:, at])
        u = dot(to_mine, pre_v[:, at_up])
        s = jax.nn.sigmoid(g)
        gs = g * s
        hid[:, at] = (gs * u).astype(BF16)
        gfac[:, at] = gate_col * u * s * (1.0 + g * (1.0 - s))
        ufac[:, at] = gate_col * gs
        return carry

    lax.fori_loop(0, ff // block, prepare, 0)
    acc[...] = jnp.zeros_like(acc)
    pick = []
    for t in range(tiles):
        r = lax.broadcasted_iota(jnp.int32, (rows_x, groups * 16), 0)
        c = lax.broadcasted_iota(jnp.int32, (rows_x, groups * 16), 1)
        pick.append(
            ((r // extra) * 16 + t * extra + r % extra == c).astype(F32).astype(BF16)
        )
    loads[1].wait()

    final = chunks - 1

    def work_ahead(n, carry):
        at = pl.ds(pl.multiple_of(n * block, block), block)
        w_at = pl.ds(pl.multiple_of(final * chunk + n * block, block), block)
        ahead[:, at] = dot(hid[...], w_v[:, w_at]).astype(BF16)
        return carry

    lax.fori_loop(0, chunk // block, work_ahead, 0)
    packed_extra = jnp.zeros((groups * 16, WIDE), F32)
    for t in range(tiles):
        packed_extra = packed_extra + lax.dot_general(
            pick[t],
            ahead[rows_main:, t * WIDE : (t + 1) * WIDE],
            (((0,), (0,)), ((), ())),
            preferred_element_type=F32,
        )
    ahead_extra[...] = packed_extra.astype(BF16)

    c_wide = c_send.shape[-1]
    c_lane = lax.broadcasted_iota(jnp.int32, (tokens, c_wide), 1)
    c_mod = (c_lane % extra).astype(F32)
    in_extra = (c_lane >= rows_main + me * 16) & (c_lane < rows_main + me * 16 + 16)
    last_at = rows_main + groups * 16 + me * extra
    in_extra = in_extra | ((c_lane >= last_at) & (c_lane < last_at + extra))
    c_lane = c_lane.astype(F32)
    me_f = me.astype(F32)
    for k in range(2):
        hit = jnp.where(c_lane == me_f * MAIN + slot[k], 1.0, 0.0)
        over = jnp.where(in_extra & (c_mod == slot[k] - MAIN), 1.0, 0.0)
        masks[k] = jnp.where(slot[k] < MAIN, hit, over)

    def wait_chunk(k):
        self_copy(k).wait()
        for d in range(1, groups):
            arrived(recv.at[k, ring(d)], recv_sem.at[k, ring(d)])

    def use_chunk(k, carry):
        rest = recv[k, :, tiles * MAIN :, :].reshape(groups * 16, WIDE)
        for t in range(tiles):
            at = slice(t * WIDE, (t + 1) * WIDE)
            lhs[0:rows_main, at] = recv[k, :, t * MAIN : (t + 1) * MAIN, :].reshape(
                rows_main, WIDE
            )
            lhs[rows_main:, at] = dot(pick[t], rest).astype(BF16)
        return carry

    def multiply(k, n):
        kat = pl.ds(pl.multiple_of(k * chunk, chunk), chunk)
        at = pl.ds(pl.multiple_of(n * block, block), block)
        new = acc[:, at] + lax.dot_general(
            lhs[...], w_v[at, kat], (((1,), (1,)), ((), ())), preferred_element_type=F32
        )
        acc[:, at] = new
        return new

    def whole_chunk(k, carry):
        wait_chunk(k)
        use_chunk(k, carry)

        def tile(n, inner):
            multiply(k, n)
            return inner

        return lax.fori_loop(0, ff // block, tile, carry)

    lax.fori_loop(0, chunks - 1, whole_chunk, 0)
    c_sum[...] = jnp.zeros_like(c_sum)

    summed = jnp.zeros((rows_all, WIDE), F32)
    for n in range(ff // WIDE):
        at = slice(n * WIDE, (n + 1) * WIDE)
        summed = summed + hid[:, at].astype(F32) * acc[:, at]
    first_extra = rows_main + groups * 16
    c_sum[0:rows_main] = summed[0:rows_main]
    c_sum[first_extra : first_extra + rows_x] = summed[rows_main:]
    wait_chunk(final)
    summed = c_sum[0:rows_main]
    for t in range(tiles):
        come = recv[final, :, t * MAIN : (t + 1) * MAIN, :].reshape(rows_main, WIDE)
        held = ahead[0:rows_main, t * WIDE : (t + 1) * WIDE]
        summed = summed + come.astype(F32) * held.astype(F32)
    c_sum[0:rows_main] = summed
    come = recv[final, :, tiles * MAIN :, :].reshape(groups * 16, WIDE)
    c_sum[rows_main:first_extra] = come.astype(F32) * ahead_extra[...].astype(F32)
    c_send[...] = jnp.sum(jnp.transpose(c_sum[...]), axis=0, keepdims=True)

    def c_copy(d):
        return pltpu.make_async_remote_copy(
            src_ref=c_send,
            dst_ref=c_recv.at[me],
            send_sem=c_ss.at[d],
            recv_sem=c_rs.at[me],
            device_id=(q, ring(d)),
            device_id_type=MESH,
        )

    for d in order:
        c_copy(d).start()
    c_recv[me] = c_send[...]

    use_chunk(final, 0)

    def last_tile(n, carry):
        multiply(final, n)
        return carry

    lax.fori_loop(0, ff // block, last_tile, 0)

    def finish(n):
        for first, factor in ((n * block, gfac), (ff + n * block, ufac)):
            back = acc[:, n * block : (n + 1) * block] * factor[:, n * block : (n + 1) * block]
            out_ref[:, first : first + block] = dot(to_natural, back.astype(BF16)).astype(BF16)

    parts = ff // block
    turns = [list(range(parts))[i::3] for i in range(3)]

    for d in range(1, groups):
        arrived(c_recv.at[ring(d)], c_rs.at[ring(d)])
    prod = []
    for k in range(2):
        found = jnp.zeros((tokens, c_wide), F32)
        for e in range(groups):
            found = found + jnp.where(ident[k] == float(e), c_recv[e], 0.0)
        prod.append(jnp.sum(found * masks[k], axis=1, keepdims=True))
    mixture = weight[0] * prod[0] + weight[1] * prod[1]
    terms = jnp.zeros((tokens, WIDE), F32)
    for k in range(2):
        grad = (prod[k] - mixture) / total * score[k] * (1.0 - score[k])
        terms = terms + onehot[k] * grad
    terms = jnp.transpose(terms)[0:groups]
    high = terms.astype(BF16).astype(F32)
    middle = (terms - high).astype(BF16).astype(F32)
    low = terms - high - middle
    stack = jnp.concatenate([high, middle, low, jnp.zeros_like(low)], axis=0).astype(BF16)
    loads[2].wait()
    for n in range(chunks):
        at = slice(n * chunk, (n + 1) * chunk)
        three = dot(stack, x_v[:, at])
        part = three[0:groups] + three[groups : 2 * groups] + three[2 * groups : 3 * groups]
        for t in range(tiles):
            y_full[:, n * tiles + t, :] = part[:, t * WIDE : (t + 1) * WIDE]
    y_send[...] = y_full[...].astype(BF16)

    def y_copy(d):
        to = ring(d)
        return pltpu.make_async_remote_copy(
            src_ref=y_send.at[to],
            dst_ref=y_recv.at[me],
            send_sem=y_ss.at[d],
            recv_sem=y_rs.at[me],
            device_id=(q, to),
            device_id_type=MESH,
        )

    for d in order:
        y_copy(d).start()
    y_recv[me] = y_send[me]
    for n in turns[0]:
        finish(n)

    def sent(k, carry):
        for d in order:
            row_copy(k, d).wait_send()
        return carry

    for d in range(1, groups):
        arrived(y_recv.at[ring(d)], y_rs.at[ring(d)])

    def total_of(buffer, count):
        together = buffer[0].astype(F32)
        for j in range(1, count):
            together = together + buffer[j].astype(F32)
        return together

    g_send[...] = total_of(y_recv, groups).astype(BF16)

    def g_copy(d):
        to, _ = mate(d)
        return pltpu.make_async_remote_copy(
            src_ref=g_send,
            dst_ref=g_recv.at[rank],
            send_sem=g_ss.at[d],
            recv_sem=g_rs.at[rank],
            device_id=(to, me),
            device_id_type=MESH,
        )

    for d in sorted(range(1, team), key=lambda d: -min(d, team - d)):
        g_copy(d).start()
    g_recv[rank] = g_send[...]
    for n in turns[1]:
        finish(n)
    for d in range(1, team):
        arrived(g_recv.at[mate(d)[1]], g_rs.at[mate(d)[1]])

    z_send[...] = total_of(g_recv, team).astype(BF16)

    def z_copy(d):
        to, _ = zmate(d)
        return pltpu.make_async_remote_copy(
            src_ref=z_send,
            dst_ref=z_recv.at[zi],
            send_sem=z_ss.at[d],
            recv_sem=z_rs.at[zi],
            device_id=(to, me),
            device_id_type=MESH,
        )

    for d in sorted(range(1, nz), key=lambda d: -min(d, nz - d)):
        z_copy(d).start()
    z_recv[zi] = z_send[...]

    lax.fori_loop(0, chunks, sent, 0)
    for d in order:
        gate_copy(d).wait_send()
        c_copy(d).wait_send()
        y_copy(d).wait_send()
    for d in range(1, team):
        g_copy(d).wait_send()
    for n in turns[2]:
        finish(n)

    for d in range(1, nz):
        arrived(z_recv.at[zmate(d)[1]], z_rs.at[zmate(d)[1]])
    row = total_of(z_recv, nz) * (1.0 / math.sqrt(tokens * nx * nz * nc * groups))
    for i in range(width // WIDE):
        router_ref[:, i * WIDE : (i + 1) * WIDE] = row[i : i + 1]
    for d in range(1, nz):
        z_copy(d).wait_send()


def hand_out(grad_in, row_in, grad_out, row_out, sem):
    rows = grad_in.shape[0]
    step = 96 if rows % 96 == 0 else rows
    copies = [pltpu.make_async_copy(row_in, row_out, sem.at[0])]
    for i in range(rows // step):
        at = slice(i * step, (i + 1) * step)
        copies.append(pltpu.make_async_copy(grad_in.at[at], grad_out.at[at], sem.at[i + 1]))
    for one in copies:
        one.start()
    for one in copies:
        one.wait()


def body(dims, normed_input, output_grad, route_logits, route_ids, down_weight, pre_act):
    groups = lax.axis_size("expert")
    tokens, width = normed_input.shape
    ff = down_weight.shape[1]
    slots = pre_act.shape[0]
    cap = slots // groups
    nx, nz, nc = dims
    team = nx * nc
    extra = cap - MAIN
    tiles = 16 // extra
    chunk = tiles * WIDE
    chunks = width // chunk
    block_rows = tiles * MAIN + 16
    lines = -(-width // (16 * WIDE)) * 16
    c_wide = groups * (MAIN + 16) + -(-groups * extra // WIDE) * WIDE
    vmem = pl.BlockSpec(memory_space=pltpu.VMEM)
    anywhere = pl.BlockSpec(memory_space=pl.ANY)
    dma = pltpu.SemaphoreType.DMA
    grad, row = pl.pallas_call(
        functools.partial(kernel, dims, groups, cap),
        out_shape=(
            pltpu.VMEM((slots, 2 * ff), BF16),
            pltpu.VMEM((1, width), F32),
        ),
        in_specs=[anywhere] * 6,
        out_specs=(vmem, vmem),
        scratch_shapes=[
            pltpu.VMEM(route_ids.shape[::-1], jnp.int32),
            pltpu.VMEM(route_logits.shape[::-1], F32),
            pltpu.VMEM((tokens, width), BF16),
            pltpu.VMEM((tokens, width), BF16),
            pltpu.VMEM((ff, width), BF16),
            pltpu.VMEM((slots, 2 * ff), BF16),
            pltpu.VMEM((chunks, groups, block_rows, WIDE), BF16),
            pltpu.VMEM((chunks, groups, block_rows, WIDE), BF16),
            pltpu.VMEM((slots, chunk), BF16),
            pltpu.VMEM((slots, ff), F32),
            pltpu.VMEM((slots, ff), BF16),
            pltpu.VMEM((slots, ff), F32),
            pltpu.VMEM((slots, ff), F32),
            pltpu.VMEM((slots, chunk), BF16),
            pltpu.VMEM((groups * 16, WIDE), BF16),
            pltpu.VMEM((2, tokens, c_wide), F32),
            pltpu.VMEM((groups, 1, WIDE), F32),
            pltpu.VMEM((groups, 1, WIDE), F32),
            pltpu.VMEM((c_wide, WIDE), F32),
            pltpu.VMEM((1, c_wide), F32),
            pltpu.VMEM((groups, 1, c_wide), F32),
            pltpu.VMEM((groups, lines, WIDE), F32),
            pltpu.VMEM((groups, lines, WIDE), BF16),
            pltpu.VMEM((groups, lines, WIDE), BF16),
            pltpu.VMEM((lines, WIDE), BF16),
            pltpu.VMEM((team, lines, WIDE), BF16),
            pltpu.VMEM((lines, WIDE), BF16),
            pltpu.VMEM((nz, lines, WIDE), BF16),
            dma((chunks,)),
            dma((5,)),
            dma((chunks, groups)),
            dma((chunks, groups)),
            dma((chunks,)),
            dma((groups,)),
            dma((groups,)),
            dma((groups,)),
            dma((groups,)),
            dma((groups,)),
            dma((groups,)),
            dma((team,)),
            dma((team,)),
            dma((nz,)),
            dma((nz,)),
        ],
        compiler_params=pltpu.CompilerParams(
            collective_id=0, has_side_effects=True, vmem_limit_bytes=56 * 1024 * 1024
        ),
        cost_estimate=pl.CostEstimate(
            flops=2 * slots * width * ff, bytes_accessed=12 * 1024 * 1024, transcendentals=0
        ),
    )(route_ids.T, route_logits.T, normed_input, output_grad, down_weight, pre_act)
    return pl.pallas_call(
        hand_out,
        out_shape=(
            jax.ShapeDtypeStruct(grad.shape, grad.dtype),
            jax.ShapeDtypeStruct(row.shape, row.dtype),
        ),
        in_specs=[vmem, vmem],
        out_specs=(anywhere, anywhere),
        scratch_shapes=[
            dma((8,)),
        ],
        cost_estimate=pl.CostEstimate(
            flops=0, bytes_accessed=4 * slots * ff * 2, transcendentals=0
        ),
    )(
        pltpu.with_memory_space_constraint(grad, pltpu.VMEM),
        pltpu.with_memory_space_constraint(row, pltpu.VMEM),
    )


def solution(mesh):
    dims = dp_dims(mesh.shape["dp"])
    return jax.shard_map(
        functools.partial(body, dims),
        mesh=mesh,
        in_specs=(
            P(("dp", "expert"), None),
            P(("dp", "expert"), None),
            P(("dp", "expert"), None),
            P(("dp", "expert"), None),
            P("expert", None, None),
            P(("dp", "expert"), None),
        ),
        out_specs=(P(("dp", "expert"), None), P("expert", None)),
        check_vma=False,
    )
```

```python
import functools
import math

import jax
import jax.numpy as jnp
from jax import lax
from jax.experimental import pallas as pl
from jax.experimental.pallas import tpu as pltpu
from jax.sharding import PartitionSpec as P

MESH = pl.DeviceIdType.MESH
F32 = jnp.float32
BF16 = jnp.bfloat16
MAIN = 32
WIDE = 128


def dot(a, b):
    return jnp.dot(a, b, preferred_element_type=F32)


def dp_dims(n_dp):
    return (4, n_dp // 8, 2)


def kernel(
    dims,
    groups,
    cap,
    ids_hbm,
    logits_hbm,
    x_hbm,
    g_hbm,
    w_hbm,
    pre_hbm,
    out_ref,
    router_ref,
    ids_ref,
    logits_ref,
    g_v,
    x_v,
    w_v,
    pre_v,
    send,
    recv,
    lhs,
    acc,
    hid,
    gfac,
    ufac,
    ahead,
    ahead_extra,
    masks,
    gate_send,
    gate_recv,
    c_sum,
    c_send,
    c_recv,
    y_full,
    y_send,
    y_recv,
    g_send,
    g_recv,
    z_send,
    z_recv,
    g_sem,
    load_sem,
    send_sem,
    recv_sem,
    self_sem,
    gate_ss,
    gate_rs,
    c_ss,
    c_rs,
    y_ss,
    y_rs,
    g_ss,
    g_rs,
    z_ss,
    z_rs,
):
    nx, nz, nc = dims
    team = nx * nc
    tokens, width = g_v.shape
    ff = w_v.shape[0]
    extra = cap - MAIN
    tiles = 16 // extra
    chunk = tiles * WIDE
    chunks = width // chunk
    rows_main = groups * MAIN
    rows_all = groups * cap

    q = lax.axis_index("dp")
    me = lax.axis_index("expert")
    core = lax.rem(q, nc)
    zi = lax.rem(q // nc, nz)
    xi = q // (nc * nz)
    rank = xi * nc + core

    def ring(d):
        return lax.rem(me + d, groups)

    def mate(d):
        r = lax.rem(rank + d, team)
        return ((r // nc) * nz + zi) * nc + lax.rem(r, nc), r

    def zmate(d):
        z = lax.rem(zi + d, nz)
        return (xi * nz + z) * nc + core, z

    ids_load = pltpu.make_async_copy(ids_hbm, ids_ref, load_sem.at[3])
    logits_load = pltpu.make_async_copy(logits_hbm, logits_ref, load_sem.at[4])
    ids_load.start()
    barrier = pltpu.get_barrier_semaphore()
    near_last = sorted(range(1, groups), key=lambda d: -min(d, groups - d))
    for d in near_last:
        pl.semaphore_signal(barrier, inc=1, device_id=(q, ring(d)), device_id_type=MESH)
    g_loads = [
        pltpu.make_async_copy(
            g_hbm.at[:, k * chunk : (k + 1) * chunk],
            g_v.at[:, k * chunk : (k + 1) * chunk],
            g_sem.at[k],
        )
        for k in range(chunks)
    ]
    for one in g_loads:
        one.start()
    for d in range(1, team):
        pl.semaphore_signal(barrier, inc=1, device_id=(mate(d)[0], me), device_id_type=MESH)
    for d in sorted(range(1, nz), key=lambda d: -min(d, nz - d)):
        pl.semaphore_signal(barrier, inc=1, device_id=(zmate(d)[0], me), device_id_type=MESH)

    logits_load.start()

    loads = [
        pltpu.make_async_copy(pre_hbm, pre_v, load_sem.at[0]),
        pltpu.make_async_copy(w_hbm.at[0], w_v, load_sem.at[1]),
        pltpu.make_async_copy(x_hbm, x_v, load_sem.at[2]),
    ]

    ids_load.wait()
    ids = ids_ref[...].astype(F32)
    expert = lax.broadcasted_iota(jnp.int32, (16, tokens), 0).astype(F32)
    onehot_t = [(ids[k : k + 1] == expert).astype(F32) for k in range(2)]
    before = (
        lax.broadcasted_iota(jnp.int32, (tokens, tokens), 0)
        < lax.broadcasted_iota(jnp.int32, (tokens, tokens), 1)
    ).astype(F32)
    count_t = dot((onehot_t[0] + onehot_t[1]).astype(BF16), before.astype(BF16))
    slot_t = [jnp.sum(o * count_t, axis=0, keepdims=True) for o in onehot_t]
    to_main, to_extra = [], []
    for k in range(2):
        inside = slot_t[k] < MAIN
        at_k = ids[k : k + 1]
        to_main.append(jnp.where(inside, at_k * MAIN + slot_t[k], -1.0))
        to_extra.append(jnp.where(inside, -1000.0, at_k * 16 + slot_t[k] - MAIN))
    row_main = lax.broadcasted_iota(jnp.int32, (rows_main, tokens), 0).astype(F32)
    row_extra = lax.broadcasted_iota(jnp.int32, (groups * 16, tokens), 0).astype(F32)
    place_main = (
        (row_main == to_main[0]).astype(F32) + (row_main == to_main[1]).astype(F32)
    ).astype(BF16)
    place_extra = [
        (
            (row_extra == to_extra[0] + extra * t).astype(F32)
            + (row_extra == to_extra[1] + extra * t).astype(F32)
        ).astype(BF16)
        for t in range(tiles)
    ]

    order = near_last

    def gate_copy(d):
        to = ring(d)
        return pltpu.make_async_remote_copy(
            src_ref=gate_send.at[to],
            dst_ref=gate_recv.at[me],
            send_sem=gate_ss.at[d],
            recv_sem=gate_rs.at[me],
            device_id=(q, to),
            device_id_type=MESH,
        )

    def row_copy(k, d):
        to = ring(d)
        return pltpu.make_async_remote_copy(
            src_ref=send.at[k, to],
            dst_ref=recv.at[k, me],
            send_sem=send_sem.at[k, d],
            recv_sem=recv_sem.at[k, me],
            device_id=(q, to),
            device_id_type=MESH,
        )

    def self_copy(k):
        return pltpu.make_async_copy(send.at[k, me], recv.at[k, me], self_sem.at[k])

    def arrived(buffer, sem):
        pltpu.make_async_copy(buffer, buffer, sem).wait()

    def fill_chunk(k):
        cols = g_v[:, pl.ds(pl.multiple_of(k * chunk, chunk), chunk)]
        main = dot(place_main, cols).astype(BF16)
        rest = jnp.zeros((groups * 16, WIDE), F32)
        for t in range(tiles):
            piece_t = main[:, t * WIDE : (t + 1) * WIDE]
            send[k, :, t * MAIN : (t + 1) * MAIN, :] = piece_t.reshape(groups, MAIN, WIDE)
            rest = rest + dot(place_extra[t], cols[:, t * WIDE : (t + 1) * WIDE])
        send[k, :, tiles * MAIN :, :] = rest.astype(BF16).reshape(groups, 16, WIDE)

    def start_chunk(k):
        for d in order:
            row_copy(k, d).start()
        self_copy(k).start()

    g_loads[0].wait()
    fill_chunk(0)
    pl.semaphore_wait(barrier, groups - 1 + team - 1 + nz - 1)
    start_chunk(0)
    for one in loads:
        one.start()

    logits_load.wait()
    scores_t = jax.nn.sigmoid(logits_ref[...])
    score_t = [scores_t[k : k + 1] for k in range(2)]
    total_t = score_t[0] + score_t[1]
    weight_t = [v / total_t for v in score_t]
    slot_row = lax.broadcasted_iota(jnp.int32, (WIDE, tokens), 0).astype(F32)
    gates = jnp.zeros((16, WIDE), F32)
    for k in range(2):
        gate = weight_t[k].astype(BF16).astype(F32)
        gates = gates + lax.dot_general(
            (onehot_t[k] * gate).astype(BF16),
            (slot_row == slot_t[k]).astype(F32).astype(BF16),
            (((1,), (1,)), ((), ())),
            preferred_element_type=F32,
        )
    for e in range(groups):
        gate_send[e] = gates[e : e + 1]
    for d in order:
        gate_copy(d).start()
    gate_recv[me] = gate_send[me]

    def send_chunk(k, carry):
        at = pl.ds(pl.multiple_of(k * chunk, chunk), chunk)
        pltpu.make_async_copy(g_hbm.at[:, at], g_v.at[:, at], g_sem.at[k]).wait()
        fill_chunk(k)
        start_chunk(k)
        return carry

    lax.fori_loop(1, chunks, send_chunk, 0)

    rows = [ids[0:1], ids[1:2], *slot_t, *score_t, *weight_t, total_t]
    rows.append(jnp.zeros((WIDE - len(rows), tokens), F32))
    columns = jnp.transpose(jnp.concatenate(rows, axis=0))
    column = [columns[:, i : i + 1] for i in range(9)]
    ident, slot, score, weight, total = (
        column[0:2],
        column[2:4],
        column[4:6],
        column[6:8],
        column[8],
    )
    lane = lax.broadcasted_iota(jnp.int32, (tokens, WIDE), 1).astype(F32)
    onehot = [(i == lane).astype(F32) for i in ident]
    y_full[...] = jnp.zeros_like(y_full)

    for d in range(1, groups):
        arrived(gate_recv.at[ring(d)], gate_rs.at[ring(d)])
    lane_m = lax.broadcasted_iota(jnp.int32, (MAIN, WIDE), 1)
    row_m = lax.broadcasted_iota(jnp.int32, (MAIN, WIDE), 0)
    rows_x = rows_all - rows_main
    lane_x = lax.broadcasted_iota(jnp.int32, (rows_x, WIDE), 1)
    row_x = lax.broadcasted_iota(jnp.int32, (rows_x, WIDE), 0)
    gate_x = jnp.zeros((rows_x, WIDE), F32)
    gate_parts = []
    for j in range(groups):
        one = gate_recv[j]
        gate_parts.append(
            jnp.sum(jnp.where(lane_m == row_m, one, 0.0), axis=1, keepdims=True)
        )
        mine = (row_x // extra == j) & (lane_x == MAIN + row_x % extra)
        gate_x = gate_x + jnp.where(mine, one, 0.0)
    gate_parts.append(jnp.sum(gate_x, axis=1, keepdims=True))
    gate_col = jnp.concatenate(gate_parts, axis=0)

    def natural(r):
        s = r - rows_main
        return jnp.where(
            r < rows_main,
            (r // MAIN) * cap + r % MAIN,
            (s // extra) * cap + MAIN + s % extra,
        )

    square_r = lax.broadcasted_iota(jnp.int32, (rows_all, rows_all), 0)
    square_c = lax.broadcasted_iota(jnp.int32, (rows_all, rows_all), 1)
    to_mine = (natural(square_r) == square_c).astype(F32).astype(BF16)
    to_natural = (natural(square_c) == square_r).astype(F32).astype(BF16)
    loads[0].wait()
    block = 256

    def prepare(n, carry):
        at = pl.ds(pl.multiple_of(n * block, block), block)
        at_up = pl.ds(pl.multiple_of(ff + n * block, block), block)
        g = dot(to_mine, pre_v[:, at])
        u = dot(to_mine, pre_v[:, at_up])
        s = jax.nn.sigmoid(g)
        gs = g * s
        hid[:, at] = (gs * u).astype(BF16)
        gfac[:, at] = gate_col * u * s * (1.0 + g * (1.0 - s))
        ufac[:, at] = gate_col * gs
        return carry

    lax.fori_loop(0, ff // block, prepare, 0)
    acc[...] = jnp.zeros_like(acc)
    pick = []
    for t in range(tiles):
        r = lax.broadcasted_iota(jnp.int32, (rows_x, groups * 16), 0)
        c = lax.broadcasted_iota(jnp.int32, (rows_x, groups * 16), 1)
        pick.append(
            ((r // extra) * 16 + t * extra + r % extra == c).astype(F32).astype(BF16)
        )
    loads[1].wait()

    final = chunks - 1

    def work_ahead(n, carry):
        at = pl.ds(pl.multiple_of(n * block, block), block)
        w_at = pl.ds(pl.multiple_of(final * chunk + n * block, block), block)
        ahead[:, at] = dot(hid[...], w_v[:, w_at]).astype(BF16)
        return carry

    lax.fori_loop(0, chunk // block, work_ahead, 0)
    packed_extra = jnp.zeros((groups * 16, WIDE), F32)
    for t in range(tiles):
        packed_extra = packed_extra + lax.dot_general(
            pick[t],
            ahead[rows_main:, t * WIDE : (t + 1) * WIDE],
            (((0,), (0,)), ((), ())),
            preferred_element_type=F32,
        )
    ahead_extra[...] = packed_extra.astype(BF16)

    c_wide = c_send.shape[-1]
    c_lane = lax.broadcasted_iota(jnp.int32, (tokens, c_wide), 1)
    c_mod = (c_lane % extra).astype(F32)
    in_extra = (c_lane >= rows_main + me * 16) & (c_lane < rows_main + me * 16 + 16)
    last_at = rows_main + groups * 16 + me * extra
    in_extra = in_extra | ((c_lane >= last_at) & (c_lane < last_at + extra))
    c_lane = c_lane.astype(F32)
    me_f = me.astype(F32)
    for k in range(2):
        hit = jnp.where(c_lane == me_f * MAIN + slot[k], 1.0, 0.0)
        over = jnp.where(in_extra & (c_mod == slot[k] - MAIN), 1.0, 0.0)
        masks[k] = jnp.where(slot[k] < MAIN, hit, over).astype(BF16)

    def wait_chunk(k):
        self_copy(k).wait()
        for d in range(1, groups):
            arrived(recv.at[k, ring(d)], recv_sem.at[k, ring(d)])

    def use_chunk(k, carry):
        rest = recv[k, :, tiles * MAIN :, :].reshape(groups * 16, WIDE)
        for t in range(tiles):
            at = slice(t * WIDE, (t + 1) * WIDE)
            lhs[0:rows_main, at] = recv[k, :, t * MAIN : (t + 1) * MAIN, :].reshape(
                rows_main, WIDE
            )
            lhs[rows_main:, at] = dot(pick[t], rest).astype(BF16)
        return carry

    def multiply(k, n):
        kat = pl.ds(pl.multiple_of(k * chunk, chunk), chunk)
        at = pl.ds(pl.multiple_of(n * block, block), block)
        new = acc[:, at] + lax.dot_general(
            lhs[...], w_v[at, kat], (((1,), (1,)), ((), ())), preferred_element_type=F32
        )
        acc[:, at] = new
        return new

    def whole_chunk(k, carry):
        wait_chunk(k)
        use_chunk(k, carry)

        def tile(n, inner):
            multiply(k, n)
            return inner

        return lax.fori_loop(0, ff // block, tile, carry)

    lax.fori_loop(0, chunks - 1, whole_chunk, 0)
    c_sum[...] = jnp.zeros_like(c_sum)

    summed = jnp.zeros((rows_all, WIDE), F32)
    for n in range(ff // WIDE):
        at = slice(n * WIDE, (n + 1) * WIDE)
        summed = summed + hid[:, at].astype(F32) * acc[:, at]
    first_extra = rows_main + groups * 16
    c_sum[0:rows_main] = summed[0:rows_main]
    c_sum[first_extra : first_extra + rows_x] = summed[rows_main:]
    wait_chunk(final)
    summed = c_sum[0:rows_main]
    for t in range(tiles):
        come = recv[final, :, t * MAIN : (t + 1) * MAIN, :].reshape(rows_main, WIDE)
        held = ahead[0:rows_main, t * WIDE : (t + 1) * WIDE]
        summed = summed + come.astype(F32) * held.astype(F32)
    c_sum[0:rows_main] = summed
    come = recv[final, :, tiles * MAIN :, :].reshape(groups * 16, WIDE)
    c_sum[rows_main:first_extra] = come.astype(F32) * ahead_extra[...].astype(F32)
    c_send[...] = jnp.sum(jnp.transpose(c_sum[...]), axis=0, keepdims=True)

    def c_copy(d):
        return pltpu.make_async_remote_copy(
            src_ref=c_send,
            dst_ref=c_recv.at[me],
            send_sem=c_ss.at[d],
            recv_sem=c_rs.at[me],
            device_id=(q, ring(d)),
            device_id_type=MESH,
        )

    for d in order:
        c_copy(d).start()
    c_recv[me] = c_send[...]

    use_chunk(final, 0)

    def last_tile(n, carry):
        multiply(final, n)
        return carry

    lax.fori_loop(0, ff // block, last_tile, 0)

    def finish(n):
        for first, factor in ((n * block, gfac), (ff + n * block, ufac)):
            back = acc[:, n * block : (n + 1) * block] * factor[:, n * block : (n + 1) * block]
            out_ref[:, first : first + block] = dot(to_natural, back.astype(BF16)).astype(BF16)

    parts = ff // block
    turns = [list(range(parts))[i::3] for i in range(3)]

    for d in range(1, groups):
        arrived(c_recv.at[ring(d)], c_rs.at[ring(d)])
    come = jnp.concatenate([c_recv[e] for e in range(groups)], axis=0)
    high = come.astype(BF16).astype(F32)
    middle = (come - high).astype(BF16).astype(F32)
    low = come - high - middle
    stack = jnp.concatenate([high, middle, low, jnp.zeros_like(low)], axis=0).astype(BF16)
    part_lane = lax.broadcasted_iota(jnp.int32, (tokens, 4 * groups), 1)
    part_lane = (part_lane % groups).astype(F32)
    prod = []
    for k in range(2):
        found = lax.dot_general(
            masks[k], stack, (((1,), (1,)), ((), ())), preferred_element_type=F32
        )
        found = jnp.where(part_lane == ident[k], found, 0.0)
        prod.append(jnp.sum(found, axis=1, keepdims=True))
    mixture = weight[0] * prod[0] + weight[1] * prod[1]
    terms = jnp.zeros((tokens, WIDE), F32)
    for k in range(2):
        grad = (prod[k] - mixture) / total * score[k] * (1.0 - score[k])
        terms = terms + onehot[k] * grad
    terms = jnp.transpose(terms)[0:groups]
    high = terms.astype(BF16).astype(F32)
    middle = (terms - high).astype(BF16).astype(F32)
    low = terms - high - middle
    stack = jnp.concatenate([high, middle, low, jnp.zeros_like(low)], axis=0).astype(BF16)
    loads[2].wait()
    for n in range(chunks):
        at = slice(n * chunk, (n + 1) * chunk)
        three = dot(stack, x_v[:, at])
        part = three[0:groups] + three[groups : 2 * groups] + three[2 * groups : 3 * groups]
        for t in range(tiles):
            y_full[:, n * tiles + t, :] = part[:, t * WIDE : (t + 1) * WIDE]
    y_send[...] = y_full[...].astype(BF16)

    def y_copy(d):
        to = ring(d)
        return pltpu.make_async_remote_copy(
            src_ref=y_send.at[to],
            dst_ref=y_recv.at[me],
            send_sem=y_ss.at[d],
            recv_sem=y_rs.at[me],
            device_id=(q, to),
            device_id_type=MESH,
        )

    for d in order:
        y_copy(d).start()
    y_recv[me] = y_send[me]
    for n in turns[0]:
        finish(n)

    def sent(k, carry):
        for d in order:
            row_copy(k, d).wait_send()
        return carry

    for d in range(1, groups):
        arrived(y_recv.at[ring(d)], y_rs.at[ring(d)])

    def total_of(buffer, count):
        together = buffer[0].astype(F32)
        for j in range(1, count):
            together = together + buffer[j].astype(F32)
        return together

    g_send[...] = total_of(y_recv, groups).astype(BF16)

    def g_copy(d):
        to, _ = mate(d)
        return pltpu.make_async_remote_copy(
            src_ref=g_send,
            dst_ref=g_recv.at[rank],
            send_sem=g_ss.at[d],
            recv_sem=g_rs.at[rank],
            device_id=(to, me),
            device_id_type=MESH,
        )

    for d in sorted(range(1, team), key=lambda d: -min(d, team - d)):
        g_copy(d).start()
    g_recv[rank] = g_send[...]
    for n in turns[1]:
        finish(n)
    for d in range(1, team):
        arrived(g_recv.at[mate(d)[1]], g_rs.at[mate(d)[1]])

    z_send[...] = total_of(g_recv, team).astype(BF16)

    def z_copy(d):
        to, _ = zmate(d)
        return pltpu.make_async_remote_copy(
            src_ref=z_send,
            dst_ref=z_recv.at[zi],
            send_sem=z_ss.at[d],
            recv_sem=z_rs.at[zi],
            device_id=(to, me),
            device_id_type=MESH,
        )

    for d in sorted(range(1, nz), key=lambda d: -min(d, nz - d)):
        z_copy(d).start()
    z_recv[zi] = z_send[...]

    lax.fori_loop(0, chunks, sent, 0)
    for d in order:
        gate_copy(d).wait_send()
        c_copy(d).wait_send()
        y_copy(d).wait_send()
    for d in range(1, team):
        g_copy(d).wait_send()
    for n in turns[2]:
        finish(n)

    for d in range(1, nz):
        arrived(z_recv.at[zmate(d)[1]], z_rs.at[zmate(d)[1]])
    row = total_of(z_recv, nz) * (1.0 / math.sqrt(tokens * nx * nz * nc * groups))
    for i in range(width // WIDE):
        router_ref[:, i * WIDE : (i + 1) * WIDE] = row[i : i + 1]
    for d in range(1, nz):
        z_copy(d).wait_send()


def hand_out(grad_in, row_in, grad_out, row_out, sem):
    rows = grad_in.shape[0]
    step = 96 if rows % 96 == 0 else rows
    copies = [pltpu.make_async_copy(row_in, row_out, sem.at[0])]
    for i in range(rows // step):
        at = slice(i * step, (i + 1) * step)
        copies.append(pltpu.make_async_copy(grad_in.at[at], grad_out.at[at], sem.at[i + 1]))
    for one in copies:
        one.start()
    for one in copies:
        one.wait()


def body(dims, normed_input, output_grad, route_logits, route_ids, down_weight, pre_act):
    groups = lax.axis_size("expert")
    tokens, width = normed_input.shape
    ff = down_weight.shape[1]
    slots = pre_act.shape[0]
    cap = slots // groups
    nx, nz, nc = dims
    team = nx * nc
    extra = cap - MAIN
    tiles = 16 // extra
    chunk = tiles * WIDE
    chunks = width // chunk
    block_rows = tiles * MAIN + 16
    lines = -(-width // (16 * WIDE)) * 16
    c_wide = groups * (MAIN + 16) + -(-groups * extra // WIDE) * WIDE
    vmem = pl.BlockSpec(memory_space=pltpu.VMEM)
    anywhere = pl.BlockSpec(memory_space=pl.ANY)
    dma = pltpu.SemaphoreType.DMA
    grad, row = pl.pallas_call(
        functools.partial(kernel, dims, groups, cap),
        out_shape=(
            pltpu.VMEM((slots, 2 * ff), BF16),
            pltpu.VMEM((1, width), F32),
        ),
        in_specs=[anywhere] * 6,
        out_specs=(vmem, vmem),
        scratch_shapes=[
            pltpu.VMEM(route_ids.shape[::-1], jnp.int32),
            pltpu.VMEM(route_logits.shape[::-1], F32),
            pltpu.VMEM((tokens, width), BF16),
            pltpu.VMEM((tokens, width), BF16),
            pltpu.VMEM((ff, width), BF16),
            pltpu.VMEM((slots, 2 * ff), BF16),
            pltpu.VMEM((chunks, groups, block_rows, WIDE), BF16),
            pltpu.VMEM((chunks, groups, block_rows, WIDE), BF16),
            pltpu.VMEM((slots, chunk), BF16),
            pltpu.VMEM((slots, ff), F32),
            pltpu.VMEM((slots, ff), BF16),
            pltpu.VMEM((slots, ff), F32),
            pltpu.VMEM((slots, ff), F32),
            pltpu.VMEM((slots, chunk), BF16),
            pltpu.VMEM((groups * 16, WIDE), BF16),
            pltpu.VMEM((2, tokens, c_wide), BF16),
            pltpu.VMEM((groups, 1, WIDE), F32),
            pltpu.VMEM((groups, 1, WIDE), F32),
            pltpu.VMEM((c_wide, WIDE), F32),
            pltpu.VMEM((1, c_wide), F32),
            pltpu.VMEM((groups, 1, c_wide), F32),
            pltpu.VMEM((groups, lines, WIDE), F32),
            pltpu.VMEM((groups, lines, WIDE), BF16),
            pltpu.VMEM((groups, lines, WIDE), BF16),
            pltpu.VMEM((lines, WIDE), BF16),
            pltpu.VMEM((team, lines, WIDE), BF16),
            pltpu.VMEM((lines, WIDE), BF16),
            pltpu.VMEM((nz, lines, WIDE), BF16),
            dma((chunks,)),
            dma((5,)),
            dma((chunks, groups)),
            dma((chunks, groups)),
            dma((chunks,)),
            dma((groups,)),
            dma((groups,)),
            dma((groups,)),
            dma((groups,)),
            dma((groups,)),
            dma((groups,)),
            dma((team,)),
            dma((team,)),
            dma((nz,)),
            dma((nz,)),
        ],
        compiler_params=pltpu.CompilerParams(
            collective_id=0, has_side_effects=True, vmem_limit_bytes=56 * 1024 * 1024
        ),
        cost_estimate=pl.CostEstimate(
            flops=2 * slots * width * ff, bytes_accessed=12 * 1024 * 1024, transcendentals=0
        ),
    )(route_ids.T, route_logits.T, normed_input, output_grad, down_weight, pre_act)
    return pl.pallas_call(
        hand_out,
        out_shape=(
            jax.ShapeDtypeStruct(grad.shape, grad.dtype),
            jax.ShapeDtypeStruct(row.shape, row.dtype),
        ),
        in_specs=[vmem, vmem],
        out_specs=(anywhere, anywhere),
        scratch_shapes=[
            dma((8,)),
        ],
        cost_estimate=pl.CostEstimate(
            flops=0, bytes_accessed=4 * slots * ff * 2, transcendentals=0
        ),
    )(
        pltpu.with_memory_space_constraint(grad, pltpu.VMEM),
        pltpu.with_memory_space_constraint(row, pltpu.VMEM),
    )


def solution(mesh):
    dims = dp_dims(mesh.shape["dp"])
    return jax.shard_map(
        functools.partial(body, dims),
        mesh=mesh,
        in_specs=(
            P(("dp", "expert"), None),
            P(("dp", "expert"), None),
            P(("dp", "expert"), None),
            P(("dp", "expert"), None),
            P("expert", None, None),
            P(("dp", "expert"), None),
        ),
        out_specs=(P(("dp", "expert"), None), P("expert", None)),
        check_vma=False,
    )
```
